32 devices in a mesh: dp: 4 (over y, core), ctx: 8 (over z, x).
Axes of the slice: x: 2, y: 2, z: 4, core: 2. Of those that a mesh axis runs over, the one named last changes fastest.
Arguments:
- span_ids: int32 [4, 16], P('dp'), may hold values from 0 to 15, as said below
- hidden_in: bfloat16 [4, 1024, 4096], P('dp', 'ctx'), may hold values from -6 to 6
- queries: bfloat16 [4, 1024, 2048], P('dp', 'ctx'), may hold values from -64 to 64
- keys_in: bfloat16 [4, 1024, 512], P('dp', 'ctx'), may hold values from -4 to 4
- values_in: bfloat16 [4, 1024, 512], P('dp', 'ctx'), may hold values from -4 to 4
- attn_out: bfloat16 [4, 1024, 2048], P('dp', 'ctx'), may hold values from -4 to 4, as said below
- out_grad: bfloat16 [4, 1024, 2048], P('dp', 'ctx'), may hold values from -6 to 6
- log_norm: float32 [4, 1024, 16], P('dp', 'ctx'), may hold values from -300 to 3000, as said below
- adapter: float32 [8, 5120], P(None, 'dp'), may hold values from -0.3 to 0.3
- moment_first: float32 [8, 5120], P(None, 'dp'), may hold values from -0.0078125 to 0.0078125
- moment_second: float32 [8, 5120], P(None, 'dp'), may hold values from 6.103516e-08 to 9.765625e-07
Outputs:
- query_grad: bfloat16 [4, 1024, 2048], P('dp', 'ctx')
- kv_grad: bfloat16 [4, 1024, 1024], P('dp', 'ctx')
- adapter_step: float32 [8, 5120], P(None, 'dp')
The draws below stay inside these ranges and needn't reach their ends.
Inputs may be any that keep to these rules, and one draw needn't show every extreme that they name: `span_ids`: in each sequence the entries 2c and 2c + 1 belong to device c of ctx; entry 2c + 1 equals 15 minus entry 2c, and the entries 2c over all c are a permutation of 0 to 7, drawn afresh for every sequence. `attn_out`: the saved softmax output of queries, keys_in and values_in under the causal mask by pos. `log_norm`: the log of the causal softmax total of each query row and head.
All inputs are finite; a program needn't handle non-finite values.
Results may differ from the reference program's by a relative error of at most 0.017.
Values may be sent and summed in bfloat16 or wider, within the bound.
A program may use at most 128 MiB of HBM per device.

```python
import math
import jax
import jax.numpy as jnp
from jax import lax

D = 4096
H = 16
KVH = 4
DH = 128
RANK = 8
ROWS = 128
HALF = 64
LENGTH = 1024
SPANS = 16
SEQS = 4
ADAPT = 5120
N_CTX = 8


def span_table(key):
    seq_keys = jax.random.split(jax.random.fold_in(key, 101), SEQS)
    order = jax.vmap(lambda seq_key: jax.random.permutation(seq_key, N_CTX))(seq_keys).astype(jnp.int32)
    paired = jnp.stack([order, 2 * N_CTX - 1 - order], axis=-1)
    return paired.reshape(SEQS, SPANS).astype(jnp.int32)


def attention_base(key):
    assignment = span_table(key)
    query_base = jax.random.truncated_normal(jax.random.fold_in(key, 202), -4.0, 4.0, (SEQS, LENGTH, H, DH), jnp.float32)
    key_base = jax.random.truncated_normal(jax.random.fold_in(key, 203), -4.0, 4.0, (SEQS, LENGTH, KVH, DH), jnp.float32)
    value_base = jax.random.truncated_normal(jax.random.fold_in(key, 204), -4.0, 4.0, (SEQS, LENGTH, KVH, DH), jnp.float32)
    queries = query_base.reshape(SEQS, LENGTH, H * DH).astype(jnp.bfloat16)
    keys_low = key_base.reshape(SEQS, LENGTH, KVH * DH).astype(jnp.bfloat16)
    values_low = value_base.reshape(SEQS, LENGTH, KVH * DH).astype(jnp.bfloat16)
    return (assignment, queries, keys_low, values_low)


def sequence_stats(seq_args):
    assignment, query_seq, key_seq, value_seq = seq_args
    row_slots = jnp.arange(LENGTH, dtype=jnp.int32)
    positions = assignment[row_slots // HALF] * HALF + row_slots % HALF
    key_heads = key_seq.reshape(LENGTH, KVH, DH).astype(jnp.float32)
    value_heads = value_seq.reshape(LENGTH, KVH, DH).astype(jnp.float32)
    block_rows = min(256, LENGTH)

    def block_stats(block_idx):
        first_row = block_idx * block_rows
        query_rows = lax.dynamic_slice_in_dim(query_seq, first_row, block_rows).reshape(block_rows, KVH, H // KVH, DH).astype(jnp.float32)
        pos_query = lax.dynamic_slice_in_dim(positions, first_row, block_rows)
        scores = jnp.einsum('rkgd,skd->kgrs', query_rows, key_heads) * DH ** (-0.5)
        visible = positions[None, :] <= pos_query[:, None]
        scores = jnp.where(visible, scores, -1e+30)
        row_top = jnp.max(scores, axis=-1, keepdims=True)
        weights = jnp.exp(scores - row_top)
        row_total = jnp.sum(weights, axis=-1, keepdims=True)
        row_norm = row_top[..., 0] + jnp.log(row_total[..., 0])
        outputs = jnp.einsum('kgrs,skd->rkgd', weights / row_total, value_heads)
        return (jnp.transpose(row_norm, (2, 0, 1)).reshape(block_rows, H), outputs.reshape(block_rows, H * DH))
    norms, outputs = lax.map(block_stats, jnp.arange(LENGTH // block_rows, dtype=jnp.int32))
    return (norms.reshape(LENGTH, H), outputs.reshape(LENGTH, H * DH).astype(jnp.bfloat16))


def attention_stats(key):
    assignment, queries, keys_low, values_low = attention_base(key)
    return lax.map(sequence_stats, (assignment, queries, keys_low, values_low))


def draw_span_ids(key, part):
    return span_table(key)


def draw_queries(key, part):
    return attention_base(key)[1]


def draw_keys_in(key, part):
    return attention_base(key)[2]


def draw_values_in(key, part):
    return attention_base(key)[3]


def draw_attn_out(key, part):
    return attention_stats(key)[1]


def draw_log_norm(key, part):
    return attention_stats(key)[0]


def draw_adapter(key, part):
    base = jax.random.truncated_normal(jax.random.fold_in(key, 305), -5.0, 5.0, (RANK, ADAPT), jnp.float32)
    factor = 1.2
    column_iota = jnp.arange(ADAPT, dtype=jnp.int32)
    column_scale = jnp.where(column_iota < D, 0.05 * factor, 0.05 / factor).astype(jnp.float32)
    return jnp.clip(base * column_scale[None, :], -0.3, 0.3).astype(jnp.float32)


def steps_of(rng, shape, shards, least, top_value):
    gain, own = 1.0, jax.random.fold_in(rng, 6)
    for position, blocks in shards:
        heights = jnp.exp(jax.random.uniform(jax.random.fold_in(own, position), (blocks,), jnp.float32, least / len(shards), top_value / len(shards)))
        gain = gain * jnp.repeat(heights, shape[position] // blocks).reshape([-1 if axis == position else 1 for axis in range(len(shape))])
    return gain


def gaussian(own_key, dims, width, limit, pieces=(), kind=jnp.bfloat16):
    array = jax.random.normal(own_key, dims, jnp.float32) * width
    if len(pieces) > 0:
        array = steps_of(own_key, dims, pieces, -0.22, 0.18) * array
    return jnp.clip(array, min=-limit, max=limit).astype(kind)


def setup_inputs(seed: int = 0) -> dict:
    seeds = jax.random.split(jax.random.key(seed), 12)
    return {
        "span_ids": draw_span_ids(jax.random.fold_in(seeds[11], 71), 0),
        "hidden_in": gaussian(seeds[1], (SEQS, LENGTH, D), 1.0, 6.0, ((0, 4), (1, 8))),
        "queries": draw_queries(jax.random.fold_in(seeds[11], 71), 0),
        "keys_in": draw_keys_in(jax.random.fold_in(seeds[11], 71), 0),
        "values_in": draw_values_in(jax.random.fold_in(seeds[11], 71), 0),
        "attn_out": draw_attn_out(jax.random.fold_in(seeds[11], 71), 0),
        "out_grad": gaussian(seeds[6], (SEQS, LENGTH, H * DH), 1.0, 6.0, ((0, 4), (1, 8))),
        "log_norm": draw_log_norm(jax.random.fold_in(seeds[11], 71), 0),
        "adapter": draw_adapter(jax.random.fold_in(seeds[11], 71), 0),
        "moment_first": gaussian(seeds[9], (RANK, ADAPT), (0.1 * (RANK * ADAPT) ** -0.5), 0.0078125, ((1, 4),), jnp.float32),
        "moment_second": jnp.clip(jnp.exp(math.log(9.765625463842298e-07) - 2.7725887 * jax.random.uniform(seeds[10], (RANK, ADAPT), jnp.float32) ** steps_of(seeds[10], (RANK, ADAPT), ((1, 4),), -0.2, 0.2)), 6.103515914901436e-08, 9.765625463842298e-07),
    }


BIAS_ONE = 1.0 - 0.9 ** 100.0
BIAS_TWO = 1.0 - 0.999 ** 100.0

def rounded(values_f32):
    low = lax.optimization_barrier(values_f32.astype(jnp.bfloat16))
    return low.astype(jnp.float32)

def grouped(rows):
    return rows.reshape(rows.shape[0], KVH, H // KVH, DH).astype(jnp.float32)

def per_head(stat_rows):
    return jnp.transpose(stat_rows.reshape(stat_rows.shape[0], KVH, H // KVH), (1, 2, 0))[..., None]

def sequence_grads(seq_args):
    assignment, query_seq, key_seq, value_seq, out_seq, grad_seq, norm_seq = seq_args
    row_slots = jnp.arange(LENGTH, dtype=jnp.int32)
    positions = assignment[row_slots // HALF] * HALF + row_slots % HALF
    key_heads = key_seq.reshape(LENGTH, KVH, DH).astype(jnp.float32)
    value_heads = value_seq.reshape(LENGTH, KVH, DH).astype(jnp.float32)
    score_scale = DH ** (-0.5)

    def device_step(kv_total, device_idx):
        first_row = device_idx * ROWS
        query_rows = grouped(lax.dynamic_slice_in_dim(query_seq, first_row, ROWS))
        grad_rows = grouped(lax.dynamic_slice_in_dim(grad_seq, first_row, ROWS))
        out_rows = grouped(lax.dynamic_slice_in_dim(out_seq, first_row, ROWS))
        norm_rows = per_head(lax.dynamic_slice_in_dim(norm_seq, first_row, ROWS))
        delta_rows = per_head(lax.optimization_barrier(jnp.sum(grad_rows * out_rows, axis=-1)).reshape(ROWS, H))
        pos_query = lax.dynamic_slice_in_dim(positions, first_row, ROWS)
        visible = positions[None, :] <= pos_query[:, None]
        scores = jnp.einsum('rkgd,skd->kgrs', query_rows, key_heads) * score_scale
        weights = jnp.where(visible, jnp.exp(scores - norm_rows), 0.0)
        weights_low = rounded(weights)
        d_weights = jnp.einsum('rkgd,skd->kgrs', grad_rows, value_heads)
        d_scores = rounded(weights * (d_weights - delta_rows))
        query_part = jnp.einsum('kgrs,skd->rkgd', d_scores, key_heads) * score_scale
        key_part = jnp.einsum('kgrs,rkgd->skd', d_scores, query_rows) * score_scale
        value_part = jnp.einsum('kgrs,rkgd->skd', weights_low, grad_rows)
        kv_part = jnp.concatenate([key_part.reshape(LENGTH, KVH * DH), value_part.reshape(LENGTH, KVH * DH)], axis=1)
        return (kv_total + rounded(kv_part), query_part.reshape(ROWS, H * DH).astype(jnp.bfloat16))
    kv_total, query_blocks = lax.scan(device_step, jnp.zeros((LENGTH, 2 * KVH * DH), jnp.float32), jnp.arange(N_CTX, dtype=jnp.int32))
    return (query_blocks.reshape(LENGTH, H * DH), kv_total.astype(jnp.bfloat16))

def reference(span_ids, hidden_in, queries, keys_in, values_in, attn_out, out_grad, log_norm, adapter, moment_first, moment_second):
    query_grad, kv_grad = lax.map(sequence_grads, (span_ids, queries, keys_in, values_in, attn_out, out_grad, log_norm))
    adapter_low = adapter.astype(jnp.bfloat16)
    down_low = adapter_low[:, :D]
    up_low = adapter_low[:, D:]
    input_rows = hidden_in.reshape(-1, D)
    kv_rows = kv_grad.reshape(-1, 2 * KVH * DH)
    mixed_up = jnp.dot(kv_rows, up_low.T, preferred_element_type=jnp.float32).astype(jnp.bfloat16)
    mixed_down = jnp.dot(input_rows, down_low.T, preferred_element_type=jnp.float32).astype(jnp.bfloat16)
    grad_down = jnp.dot(mixed_up.T, input_rows, preferred_element_type=jnp.float32)
    grad_up = jnp.dot(mixed_down.T, kv_rows, preferred_element_type=jnp.float32)
    grad_whole = jnp.concatenate([grad_down, grad_up], axis=1)
    squares = jnp.sum(grad_whole * grad_whole)
    clip_factor = jnp.minimum(1.0, 1.0 / jnp.sqrt(squares + 1e-06))
    scaled = grad_whole * clip_factor
    moment_new = 0.9 * moment_first + 0.1 * scaled
    second_new = 0.999 * moment_second + 0.001 * scaled * scaled
    adapter_step = moment_new / BIAS_ONE / (jnp.sqrt(second_new / BIAS_TWO) + 1e-08)
    return (query_grad, kv_grad, adapter_step)
```

```python
import functools

import jax
import jax.numpy as jnp
from jax import lax
from jax.experimental import pallas as pl
from jax.experimental.pallas import tpu as pltpu
from jax.sharding import PartitionSpec as P

D = 4096
H = 16
KVH = 4
DH = 128
ROWS = 128
HALF = 64
GROUP = H // KVH
MINE = KVH // 2
CHUNK = 2 * ROWS
SCALE = DH ** (-0.5)
BIAS_ONE = 1.0 - 0.9**100.0
BIAS_TWO = 1.0 - 0.999**100.0
F32 = jnp.float32
BF16 = jnp.bfloat16


def dot_nn(a, b):
    return jnp.dot(a, b, preferred_element_type=F32)


def dot_nt(a, b):
    return lax.dot_general(a, b, (((1,), (1,)), ((), ())), preferred_element_type=F32)


def dot_tn(a, b):
    return lax.dot_general(a, b, (((0,), (0,)), ((), ())), preferred_element_type=F32)


def lanes(start, width):
    return pl.ds(pl.multiple_of(start, DH), width)


def send(src, dst, send_sem, recv_sem, **target):
    return pltpu.make_async_remote_copy(
        src_ref=src,
        dst_ref=dst,
        send_sem=send_sem,
        recv_sem=recv_sem,
        device_id=target,
        device_id_type=pl.DeviceIdType.MESH,
    )


def kernel(
    n_dp, n_ctx,
    span_ref, hid_ref, q_ref, k_ref, v_ref, o_ref, do_ref, ln_ref, ad_ref, m1_ref, m2_ref,
    dq_out, kv_out, step_out,
    kv_all, q_nbr, do_nbr, stat, stat_nbr, q_st, do_st, ln_row, de_row, dq_t,
    d_send, d_recv, dq_send, dq_recv, kx_send, kx_recv,
    ad_all, g_send, g_recv, c_recv, sq_recv,
    xk_s, xk_r, xq_s, xq_r, st_s, st_r, z_s, z_r, d_s, d_r, dq_s, dq_r, kx_s, kx_r,
    ad_s, ad_r, g_s, g_r, c_s, c_r, sq_s, sq_r,
):
    me_dp = lax.axis_index("dp")
    me = lax.axis_index("ctx")
    n_z = n_ctx // 2
    z, x = me // 2, lax.rem(me, 2)
    other = 1 - x
    nbr = 2 * z + other
    width = ad_ref.shape[1]
    fold = width // 2

    barrier = pltpu.get_barrier_semaphore()
    for step in range(1, n_ctx):
        pl.semaphore_signal(barrier, inc=1, device_id={"ctx": lax.rem(me + step, n_ctx)},
                            device_id_type=pl.DeviceIdType.MESH)
    for step in range(1, n_dp):
        pl.semaphore_signal(barrier, inc=1, device_id={"dp": lax.rem(me_dp + step, n_dp)},
                            device_id_type=pl.DeviceIdType.MESH)
    pl.semaphore_wait(barrier, n_ctx - 1 + n_dp - 1)

    def row_half(part):
        return pl.ds(pl.multiple_of(part * ROWS, ROWS), ROWS)

    sources = (k_ref, v_ref)
    sends = []

    def start(copy):
        copy.start()
        sends.append(copy)

    x_kv = []
    for h in range(MINE):
        for w in range(2):
            copy = send(
                sources[w].at[0, :, lanes((MINE * other + h) * DH, DH)],
                kv_all.at[h, z, w, row_half(x), :],
                xk_s.at[h, w], xk_r.at[h, w], ctx=nbr,
            )
            start(copy)
    for h in range(MINE):
        for w in range(2):
            kv_all[h, z, w, row_half(x), :] = sources[w][0, :, lanes((MINE * x + h) * DH, DH)]

    def z_copy(h, part, owner, peer, step, rows):
        return send(
            kv_all.at[h, owner, :, rows, :], kv_all.at[h, owner, :, rows, :],
            z_s.at[h, part, step], z_r.at[h, part, owner], ctx=2 * peer + x,
        )

    def z_push(h, part):
        rows = row_half(x if part == 0 else other)
        for step in range(1, n_z):
            start(z_copy(h, part, z, lax.rem(z + step, n_z), step, rows))

    for h in range(MINE):
        z_push(h, 0)
    heads = GROUP * DH
    for h in range(MINE):
        cols = lanes((MINE * other + h) * heads, heads)
        start(send(q_ref.at[0, :, cols], q_nbr.at[h], xq_s.at[h, 0], xq_r.at[h, 0], ctx=nbr))
        start(send(do_ref.at[0, :, cols], do_nbr.at[h], xq_s.at[h, 1], xq_r.at[h, 1], ctx=nbr))
    for step in range(1, n_dp):
        peer = lax.rem(me_dp + step, n_dp)
        start(send(ad_ref, ad_all.at[me_dp], ad_s.at[step], ad_r.at[me_dp], dp=peer))
    ad_all[me_dp] = ad_ref[...]

    ln_t = ln_ref[0].T
    per = H // 2
    for part in range(2):
        stat[part, 0:per, :] = ln_t[part * per : (part + 1) * per, :]
    for head in range(H):
        cols = slice(head * DH, (head + 1) * DH)
        prod = do_ref[0, :, cols].astype(F32) * o_ref[0, :, cols].astype(F32)
        at = per + head % per
        stat[head // per, at : at + 1, :] = jnp.sum(prod.T, axis=0, keepdims=True)
    start(send(stat.at[other], stat_nbr, st_s.at[0], st_r.at[0], ctx=nbr))

    for h in range(MINE):
        for w in range(2):
            send(
                sources[w].at[0, :, lanes((MINE * other + h) * DH, DH)],
                kv_all.at[h, z, w, row_half(other), :],
                xk_s.at[h, w], xk_r.at[h, w], ctx=nbr,
            ).wait_recv()
        z_push(h, 1)

    for h in range(MINE):
        for g in range(GROUP):
            rows = slice(g * ROWS, (g + 1) * ROWS)
            cols = lanes((x * per + h * GROUP + g) * DH, DH)
            q_st[h, rows, :] = q_ref[0, :, cols]
            do_st[h, rows, :] = do_ref[0, :, cols]

    for step in range(1, n_dp):
        src = lax.rem(me_dp + step, n_dp)
        send(ad_ref, ad_all.at[src], ad_s.at[step], ad_r.at[src], dp=src).wait_recv()
    adapter_low = jnp.concatenate([ad_all[d] for d in range(n_dp)], axis=1).astype(BF16)
    hidden = hid_ref.at[0]
    mixed_down = dot_nt(adapter_low[:, :D], hidden[...]).astype(BF16)

    send(stat.at[other], stat_nbr, st_s.at[0], st_r.at[0], ctx=nbr).wait_recv()
    for h in range(MINE):
        for g in range(GROUP):
            at = h * GROUP + g
            own = slice(g * ROWS, (g + 1) * ROWS)
            far = slice((GROUP + g) * ROWS, (GROUP + g + 1) * ROWS)
            ln_row[h, :, own] = stat[x, at : at + 1, :]
            ln_row[h, :, far] = stat_nbr[at : at + 1, :]
            de_row[h, :, own] = stat[x, per + at : per + at + 1, :]
            de_row[h, :, far] = stat_nbr[per + at : per + at + 1, :]

    lane_row = lax.rem(lax.broadcasted_iota(jnp.int32, (1, CHUNK), 1), ROWS)
    key_row = lax.broadcasted_iota(jnp.int32, (2 * ROWS, 1), 0)

    def query_pos(device):
        first, second = span_ref[0, 2 * device], span_ref[0, 2 * device + 1]
        return jnp.where(lane_row < HALF, first * HALF + lane_row, second * HALF + lane_row - HALF)

    pos_own, pos_far = query_pos(me), query_pos(nbr)
    chunks = 2 * GROUP * ROWS // CHUNK

    def d_copy(h, owner, dest, step):
        return send(d_send.at[h, dest], d_recv.at[h, owner], d_s.at[h, step], d_r.at[h, owner],
                    ctx=2 * dest + x)

    for h in range(MINE):
        for w, (src, dst) in enumerate(((q_ref, q_nbr), (do_ref, do_nbr))):
            send(src.at[0, :, lanes((MINE * other + h) * heads, heads)], dst.at[h],
                 xq_s.at[h, w], xq_r.at[h, w], ctx=nbr).wait_recv()
        for g in range(GROUP):
            rows = slice((GROUP + g) * ROWS, (GROUP + g + 1) * ROWS)
            cols = slice(g * DH, (g + 1) * DH)
            q_st[h, rows, :] = q_nbr[h, :, cols]
            do_st[h, rows, :] = do_nbr[h, :, cols]
        dq_t[h] = jnp.zeros(dq_t.shape[1:], F32)

        def block(step, carry, h=h):
            t = lax.rem(z + step, n_z)

            @pl.when(step > 0)
            def _():
                z_copy(h, 0, t, z, step, row_half(x)).wait_recv()
                z_copy(h, 1, t, z, step, row_half(other)).wait_recv()

            keys, values = kv_all[h, t, 0], kv_all[h, t, 1]
            pos_key = jnp.zeros_like(key_row)
            for s in range(4):
                base = (span_ref[0, 4 * t + s] - s) * HALF
                pos_key = jnp.where(key_row // HALF == s, base + key_row, pos_key)
            dk = jnp.zeros((2 * ROWS, DH), F32)
            dv = jnp.zeros((2 * ROWS, DH), F32)
            for j in range(chunks):
                cols = slice(j * CHUNK, (j + 1) * CHUNK)
                q_rows, do_rows = q_st[h, cols, :], do_st[h, cols, :]
                scores = dot_nt(keys, q_rows) * SCALE
                visible = pos_key <= (pos_own if j < chunks // 2 else pos_far)
                weights = jnp.where(visible, jnp.exp(scores - ln_row[h, :, cols]), 0.0)
                d_weights = dot_nt(values, do_rows)
                d_scores = (weights * (d_weights - de_row[h, :, cols])).astype(BF16)
                dv = dv + dot_nn(weights.astype(BF16), do_rows)
                dk = dk + dot_nn(d_scores, q_rows)
                dq_t[h, :, cols] += dot_tn(keys, d_scores)
            d_send[h, t, 0] = (dk * SCALE).astype(BF16)
            d_send[h, t, 1] = dv.astype(BF16)

            @pl.when(step > 0)
            def _():
                d_copy(h, z, t, step).start()

            return carry

        lax.fori_loop(0, n_z, block, 0)

        for g in range(GROUP):
            far = slice((GROUP + g) * ROWS, (GROUP + g + 1) * ROWS)
            dq_send[h, :, g * DH : (g + 1) * DH] = (dq_t[h, :, far].T * SCALE).astype(BF16)
        start(send(dq_send.at[h], dq_recv.at[h], dq_s.at[h], dq_r.at[h], ctx=nbr))
        for g in range(GROUP):
            own = slice(g * ROWS, (g + 1) * ROWS)
            dq_out[0, :, lanes((x * per + h * GROUP + g) * DH, DH)] = (
                dq_t[h, :, own].T * SCALE
            ).astype(BF16)

    kv_width = KVH * DH
    for h in range(MINE):
        d_recv[h, z] = d_send[h, z]
        for step in range(1, n_z):
            t = lax.rem(z + step, n_z)
            d_copy(h, t, z, step).wait_recv()
        for w in range(2):
            def total(rows):
                acc = d_recv[h, 0, w, rows, :].astype(F32)
                for t in range(1, n_z):
                    acc = acc + d_recv[h, t, w, rows, :].astype(F32)
                return acc.astype(BF16)

            kx_send[h, w] = total(row_half(other))
            kv_out[0, :, lanes(w * kv_width + (MINE * x + h) * DH, DH)] = total(row_half(x))
        start(send(kx_send.at[h], kx_recv.at[h], kx_s.at[h], kx_r.at[h], ctx=nbr))
    for h in range(MINE):
        send(kx_send.at[h], kx_recv.at[h], kx_s.at[h], kx_r.at[h], ctx=nbr).wait_recv()
        for w in range(2):
            kv_out[0, :, lanes(w * kv_width + (MINE * other + h) * DH, DH)] = kx_recv[h, w]

    kv_low = kv_out[0]
    mixed_up = dot_nt(adapter_low[:, D:], kv_low).astype(BF16)
    grad = jnp.concatenate([dot_nn(mixed_up, hidden[...]), dot_nn(mixed_down, kv_low)], axis=1)

    def folded(block):
        return jnp.concatenate([block[:, :fold], block[:, fold:]], axis=0).astype(BF16)

    for d in range(n_dp):
        g_send[d] = folded(grad[:, d * width : (d + 1) * width])
    for step in range(1, n_dp):
        peer = lax.rem(me_dp + step, n_dp)
        start(send(g_send.at[peer], g_recv.at[me_dp], g_s.at[step], g_r.at[me_dp], dp=peer))
    g_recv[me_dp] = g_send[me_dp]

    for h in range(MINE):
        send(dq_send.at[h], dq_recv.at[h], dq_s.at[h], dq_r.at[h], ctx=nbr).wait_recv()
        dq_out[0, :, lanes((MINE * other + h) * heads, heads)] = dq_recv[h]

    for step in range(1, n_dp):
        src = lax.rem(me_dp + step, n_dp)
        send(g_send.at[src], g_recv.at[src], g_s.at[step], g_r.at[src], dp=src).wait_recv()
    part = g_recv[0].astype(F32)
    for d in range(1, n_dp):
        part = part + g_recv[d].astype(F32)
    c_recv[me] = part.astype(BF16)
    for step in range(1, n_ctx):
        peer = lax.rem(me + step, n_ctx)
        start(send(c_recv.at[me], c_recv.at[me], c_s.at[step], c_r.at[me], ctx=peer))
    for step in range(1, n_ctx):
        src = lax.rem(me + step, n_ctx)
        send(c_recv.at[src], c_recv.at[src], c_s.at[step], c_r.at[src], ctx=src).wait_recv()
    whole = c_recv[0].astype(F32)
    for c in range(1, n_ctx):
        whole = whole + c_recv[c].astype(F32)
    grad_own = jnp.concatenate([whole[: whole.shape[0] // 2], whole[whole.shape[0] // 2 :]], axis=1)
    squares = jnp.sum(grad_own * grad_own, axis=(0, 1), keepdims=True)
    sq_recv[me_dp] = jnp.broadcast_to(squares, sq_recv.shape[1:])
    for step in range(1, n_dp):
        peer = lax.rem(me_dp + step, n_dp)
        start(send(sq_recv.at[me_dp], sq_recv.at[me_dp], sq_s.at[step], sq_r.at[me_dp], dp=peer))
    for step in range(1, n_dp):
        src = lax.rem(me_dp + step, n_dp)
        send(sq_recv.at[src], sq_recv.at[src], sq_s.at[step], sq_r.at[src], dp=src).wait_recv()
    total_sq = sq_recv[0]
    for d in range(1, n_dp):
        total_sq = total_sq + sq_recv[d]
    clip = jnp.minimum(1.0, 1.0 / jnp.sqrt(total_sq + 1e-06))[0:1, 0:1]
    scaled = grad_own * clip
    moment = 0.9 * m1_ref[...] + 0.1 * scaled
    second = 0.999 * m2_ref[...] + 0.001 * scaled * scaled
    step_out[...] = moment / BIAS_ONE / (jnp.sqrt(second / BIAS_TWO) + 1e-08)

    for copy in sends:
        copy.wait_send()
    for h in range(MINE):
        for step in range(1, n_z):
            d_copy(h, z, lax.rem(z + step, n_z), step).wait_send()


def per_device(n_dp, n_ctx, *args):
    adapter = args[8]
    rank, width = adapter.shape
    n_z = n_ctx // 2
    heads = GROUP * DH
    stack = 2 * GROUP * ROWS
    dma = pltpu.SemaphoreType.DMA
    vmem = pl.BlockSpec(memory_space=pltpu.VMEM)
    fold = (2 * rank, width // 2)
    return pl.pallas_call(
        functools.partial(kernel, n_dp, n_ctx),
        out_shape=(
            jax.ShapeDtypeStruct((1, ROWS, H * DH), BF16),
            jax.ShapeDtypeStruct((1, ROWS, 2 * KVH * DH), BF16),
            jax.ShapeDtypeStruct((rank, width), F32),
        ),
        in_specs=[pl.BlockSpec(memory_space=pltpu.SMEM)] + [vmem] * 10,
        out_specs=(vmem, vmem, vmem),
        scratch_shapes=[
            pltpu.VMEM((MINE, n_z, 2, 2 * ROWS, DH), BF16),
            pltpu.VMEM((MINE, ROWS, heads), BF16),
            pltpu.VMEM((MINE, ROWS, heads), BF16),
            pltpu.VMEM((2, H, ROWS), F32),
            pltpu.VMEM((H, ROWS), F32),
            pltpu.VMEM((MINE, stack, DH), BF16),
            pltpu.VMEM((MINE, stack, DH), BF16),
            pltpu.VMEM((MINE, 1, stack), F32),
            pltpu.VMEM((MINE, 1, stack), F32),
            pltpu.VMEM((MINE, DH, stack), F32),
            pltpu.VMEM((MINE, n_z, 2, 2 * ROWS, DH), BF16),
            pltpu.VMEM((MINE, n_z, 2, 2 * ROWS, DH), BF16),
            pltpu.VMEM((MINE, ROWS, heads), BF16),
            pltpu.VMEM((MINE, ROWS, heads), BF16),
            pltpu.VMEM((MINE, 2, ROWS, DH), BF16),
            pltpu.VMEM((MINE, 2, ROWS, DH), BF16),
            pltpu.VMEM((n_dp, rank, width), F32),
            pltpu.VMEM((n_dp,) + fold, BF16),
            pltpu.VMEM((n_dp,) + fold, BF16),
            pltpu.VMEM((n_ctx,) + fold, BF16),
            pltpu.VMEM((n_dp, 8, 128), F32),
            dma((MINE, 2)), dma((MINE, 2)),
            dma((MINE, 2)), dma((MINE, 2)),
            dma((1,)), dma((1,)),
            dma((MINE, 2, n_z)), dma((MINE, 2, n_z)),
            dma((MINE, n_z)), dma((MINE, n_z)),
            dma((MINE,)), dma((MINE,)),
            dma((MINE,)), dma((MINE,)),
            dma((n_dp,)), dma((n_dp,)),
            dma((n_dp,)), dma((n_dp,)),
            dma((n_ctx,)), dma((n_ctx,)),
            dma((n_dp,)), dma((n_dp,)),
        ],
        compiler_params=pltpu.CompilerParams(
            collective_id=0, has_side_effects=True, vmem_limit_bytes=48 * 2**20
        ),
        cost_estimate=pl.CostEstimate(flops=3 * 10**9, bytes_accessed=4 * 2**20, transcendentals=2**21),
    )(*args)


def solution(mesh):
    rows = P("dp", "ctx", None)
    columns = P(None, "dp")
    return jax.shard_map(
        functools.partial(per_device, mesh.shape["dp"], mesh.shape["ctx"]),
        mesh=mesh,
        in_specs=(P("dp", None),) + (rows,) * 7 + (columns,) * 3,
        out_specs=(rows, rows, columns),
        check_vma=False,
    )
```

```python
import functools

import jax
import jax.numpy as jnp
from jax import lax
from jax.experimental import pallas as pl
from jax.experimental.pallas import tpu as pltpu
from jax.sharding import PartitionSpec as P

D = 4096
H = 16
KVH = 4
DH = 128
ROWS = 128
HALF = 64
GROUP = H // KVH
MINE = KVH // 2
CHUNK = 2 * ROWS
SCALE = DH ** (-0.5)
BIAS_ONE = 1.0 - 0.9**100.0
BIAS_TWO = 1.0 - 0.999**100.0
F32 = jnp.float32
BF16 = jnp.bfloat16


def dot_nn(a, b):
    return jnp.dot(a, b, preferred_element_type=F32)


def dot_nt(a, b):
    return lax.dot_general(a, b, (((1,), (1,)), ((), ())), preferred_element_type=F32)


def dot_tn(a, b):
    return lax.dot_general(a, b, (((0,), (0,)), ((), ())), preferred_element_type=F32)


def lanes(start, width):
    return pl.ds(pl.multiple_of(start, DH), width)


def send(src, dst, send_sem, recv_sem, **target):
    return pltpu.make_async_remote_copy(
        src_ref=src,
        dst_ref=dst,
        send_sem=send_sem,
        recv_sem=recv_sem,
        device_id=target,
        device_id_type=pl.DeviceIdType.MESH,
    )


def kernel(
    n_dp, n_ctx,
    span_ref, hid_ref, q_ref, k_ref, v_ref, o_ref, do_ref, ln_ref, ad_ref, m1_ref, m2_ref,
    dq_out, kv_out, step_out,
    kv_all, stat, stat_nbr, q_st, do_st, ln_row, de_row, dq_t,
    d_send, d_recv, dq_send, dq_recv, kx_send, kx_recv,
    ad_all, g_send, g_recv, c_recv, sq_recv,
    hid_v, o_v, do_v, ln_v, m1_v, m2_v,
    xk_s, xk_r, xq_s, xq_r, st_s, st_r, z_s, z_r, d_s, d_r, dq_s, dq_r, kx_s, kx_r,
    ad_s, ad_r, g_s, g_r, c_s, c_r, sq_s, sq_r, l_kv, l_q, l_s,
):
    me_dp = lax.axis_index("dp")
    me = lax.axis_index("ctx")
    n_z = n_ctx // 2
    z, x = me // 2, lax.rem(me, 2)
    other = 1 - x
    nbr = 2 * z + other
    width = ad_ref.shape[1]
    fold = width // 2
    per = H // 2
    heads = GROUP * DH
    sources = (k_ref, v_ref)
    sends = []

    def start(copy):
        copy.start()
        sends.append(copy)

    def row_half(part):
        return pl.ds(pl.multiple_of(part * ROWS, ROWS), ROWS)

    own_kv = [
        [
            pltpu.make_async_copy(
                sources[w].at[0, :, lanes((MINE * x + h) * DH, DH)],
                kv_all.at[h, z, w, row_half(x), :],
                l_kv.at[h, w],
            )
            for w in range(2)
        ]
        for h in range(MINE)
    ]
    own_q = [
        pltpu.make_async_copy(
            src.at[0, :, lanes((x * per + h * GROUP + g) * DH, DH)],
            dst.at[h, g * ROWS : (g + 1) * ROWS, :],
            l_q.at[h, w, g],
        )
        for h in range(MINE)
        for w, (src, dst) in enumerate(((q_ref, q_st), (do_ref, do_st)))
        for g in range(GROUP)
    ]
    own_rest = [
        pltpu.make_async_copy(src, dst, l_s.at[i])
        for i, (src, dst) in enumerate((
            (do_ref.at[0], do_v), (o_ref.at[0], o_v), (ln_ref.at[0], ln_v),
            (ad_ref, ad_all.at[me_dp]), (hid_ref.at[0], hid_v), (m1_ref, m1_v), (m2_ref, m2_v),
        ))
    ]
    for copy in own_kv[0] + own_kv[1] + own_rest[:4] + own_q + own_rest[4:]:
        copy.start()

    barrier = pltpu.get_barrier_semaphore()
    for step in range(1, n_ctx):
        pl.semaphore_signal(barrier, inc=1, device_id={"ctx": lax.rem(me + step, n_ctx)},
                            device_id_type=pl.DeviceIdType.MESH)
    for step in range(1, n_dp):
        pl.semaphore_signal(barrier, inc=1, device_id={"dp": lax.rem(me_dp + step, n_dp)},
                            device_id_type=pl.DeviceIdType.MESH)
    pl.semaphore_wait(barrier, n_ctx - 1 + n_dp - 1)

    def x_kv(h, w, part):
        return send(
            sources[w].at[0, :, lanes((MINE * other + h) * DH, DH)],
            kv_all.at[h, z, w, row_half(part), :],
            xk_s.at[h, w], xk_r.at[h, w], ctx=nbr,
        )

    def x_q(h, w, g):
        src, dst = ((q_ref, q_st), (do_ref, do_st))[w]
        return send(
            src.at[0, :, lanes((other * per + h * GROUP + g) * DH, DH)],
            dst.at[h, (GROUP + g) * ROWS : (GROUP + g + 1) * ROWS, :],
            xq_s.at[h, w, g], xq_r.at[h, w, g], ctx=nbr,
        )

    def next_z(way):
        return z + 1 if way == 0 else z - 1

    def has_next(way):
        return z < n_z - 1 if way == 0 else z > 0

    def z_copy(h, part, owner, way):
        rows = row_half(x if part == 0 else other)
        return send(
            kv_all.at[h, owner, :, rows, :], kv_all.at[h, owner, :, rows, :],
            z_s.at[h, part, way, owner], z_r.at[h, part, owner], ctx=2 * next_z(way) + x,
        )

    def z_push(h, part):
        for way in range(2):
            @pl.when(has_next(way))
            def _(way=way):
                z_copy(h, part, z, way).start()

    def z_relay(h, distance):
        for part in range(2):
            for way in range(2):
                owner = z - distance if way == 0 else z + distance

                @pl.when((owner >= 0) & (owner < n_z))
                def _(part=part, way=way, owner=owner):
                    z_copy(h, part, owner, way).wait_recv()

                    @pl.when(has_next(way))
                    def _():
                        z_copy(h, part, owner, way).start()

    for h in range(MINE):
        for w in range(2):
            start(x_kv(h, w, x))
    for copy in own_kv[0]:
        copy.wait()
    z_push(0, 0)
    for w in range(2):
        for g in range(GROUP):
            start(x_q(0, w, g))
    for step in range(1, n_dp):
        peer = lax.rem(me_dp + step, n_dp)
        start(send(ad_ref, ad_all.at[me_dp], ad_s.at[step], ad_r.at[me_dp], dp=peer))

    for copy in own_rest[:4]:
        copy.wait()
    for part in range(2):
        stat[part, 0:per, :] = ln_v[part * per : (part + 1) * per, :]
    for head in range(H):
        cols = slice(head * DH, (head + 1) * DH)
        prod = do_v[:, cols].astype(F32) * o_v[:, cols].astype(F32)
        at = per + head % per
        stat[head // per, at : at + 1, :] = jnp.sum(prod.T, axis=0, keepdims=True)
    start(send(stat.at[other], stat_nbr, st_s.at[0], st_r.at[0], ctx=nbr))
    for w in range(2):
        for g in range(GROUP):
            start(x_q(1, w, g))

    for w in range(2):
        x_kv(0, w, other).wait_recv()
    z_push(0, 1)
    z_relay(0, 1)
    for copy in own_kv[1]:
        copy.wait()
    z_push(1, 0)
    for w in range(2):
        x_kv(1, w, other).wait_recv()
    z_push(1, 1)

    @pl.when(z == 0)
    def _():
        for h in range(MINE):
            d_recv[h, 0, z] = jnp.zeros(d_recv.shape[3:], BF16)

    @pl.when(z == n_z - 1)
    def _():
        for h in range(MINE):
            d_recv[h, 1, z] = jnp.zeros(d_recv.shape[3:], BF16)

    for copy in own_rest[4:] + own_q:
        copy.wait()
    for step in range(1, n_dp):
        src = lax.rem(me_dp + step, n_dp)
        send(ad_ref, ad_all.at[src], ad_s.at[step], ad_r.at[src], dp=src).wait_recv()
    adapter_low = jnp.concatenate([ad_all[d] for d in range(n_dp)], axis=1).astype(BF16)
    mixed_down = dot_nt(adapter_low[:, :D], hid_v[...]).astype(BF16)

    for distance in range(2, n_z):
        z_relay(0, distance)

    send(stat.at[other], stat_nbr, st_s.at[0], st_r.at[0], ctx=nbr).wait_recv()
    for h in range(MINE):
        for g in range(GROUP):
            at = h * GROUP + g
            own = slice(g * ROWS, (g + 1) * ROWS)
            far = slice((GROUP + g) * ROWS, (GROUP + g + 1) * ROWS)
            ln_row[h, :, own] = stat[x, at : at + 1, :]
            ln_row[h, :, far] = stat_nbr[at : at + 1, :]
            de_row[h, :, own] = stat[x, per + at : per + at + 1, :]
            de_row[h, :, far] = stat_nbr[per + at : per + at + 1, :]

    lane_row = lax.rem(lax.broadcasted_iota(jnp.int32, (1, CHUNK), 1), ROWS)
    key_row = lax.broadcasted_iota(jnp.int32, (2 * ROWS, 1), 0)

    def query_pos(device):
        first, second = span_ref[0, 2 * device], span_ref[0, 2 * device + 1]
        return jnp.where(lane_row < HALF, first * HALF + lane_row, second * HALF + lane_row - HALF)

    pos_own, pos_far = query_pos(me), query_pos(nbr)
    chunks = 2 * GROUP * ROWS // CHUNK

    def d_copy(h, dest, way):
        return send(d_send.at[h, dest], d_recv.at[h, way, dest], d_s.at[h, dest],
                    d_r.at[h, way, dest], ctx=2 * next_z(way) + x)

    def hops(h, step, lag):
        for way in range(2):
            before = z if way == 0 else n_z - 1 - z
            turn = step - lag * (before - 1)
            dest = n_z - 1 - turn if way == 0 else turn
            ahead = dest > z if way == 0 else dest < z

            @pl.when((before > 0) & (turn >= 0) & ahead)
            def _(way=way, dest=dest):
                d_copy(h, dest, way).wait_recv()
                both = d_send[h, dest].astype(F32) + d_recv[h, way, dest].astype(F32)
                d_send[h, dest] = both.astype(BF16)
                d_copy(h, dest, way).start()

    for h in range(MINE):
        for w in range(2):
            for g in range(GROUP):
                x_q(h, w, g).wait_recv()
        dq_t[h] = jnp.zeros(dq_t.shape[1:], F32)

        def block(step, carry, h=h):
            t = jnp.where(lax.rem(step, 2) == 0, n_z - 1 - step // 2, step // 2)
            keys, values = kv_all[h, t, 0], kv_all[h, t, 1]
            pos_key = jnp.zeros_like(key_row)
            for s in range(4):
                base = (span_ref[0, 4 * t + s] - s) * HALF
                pos_key = jnp.where(key_row // HALF == s, base + key_row, pos_key)
            dk = jnp.zeros((2 * ROWS, DH), F32)
            dv = jnp.zeros((2 * ROWS, DH), F32)
            for j in range(chunks):
                cols = slice(j * CHUNK, (j + 1) * CHUNK)
                q_rows, do_rows = q_st[h, cols, :], do_st[h, cols, :]
                scores = dot_nt(keys, q_rows) * SCALE
                visible = pos_key <= (pos_own if j < chunks // 2 else pos_far)
                weights = jnp.where(visible, jnp.exp(scores - ln_row[h, :, cols]), 0.0)
                d_weights = dot_nt(values, do_rows)
                d_scores = (weights * (d_weights - de_row[h, :, cols])).astype(BF16)
                dv = dv + dot_nn(weights.astype(BF16), do_rows)
                dk = dk + dot_nn(d_scores, q_rows)
                dq_t[h, :, cols] += dot_tn(keys, d_scores)
            d_send[h, t, 0] = (dk * SCALE).astype(BF16)
            d_send[h, t, 1] = dv.astype(BF16)

            @pl.when((z == 0) & (t > z))
            def _():
                d_copy(h, t, 0).start()

            @pl.when((z == n_z - 1) & (t < z))
            def _():
                d_copy(h, t, 1).start()

            if h == 0:
                @pl.when(step > 0)
                def _():
                    z_relay(1, step)
            else:
                hops(0, step, 2)
            return carry

        lax.fori_loop(0, n_z, block, 0)

        for g in range(GROUP):
            far = slice((GROUP + g) * ROWS, (GROUP + g + 1) * ROWS)
            dq_send[h, :, g * DH : (g + 1) * DH] = (dq_t[h, :, far].T * SCALE).astype(BF16)
        start(send(dq_send.at[h], dq_recv.at[h], dq_s.at[h], dq_r.at[h], ctx=nbr))
        for g in range(GROUP):
            own = slice(g * ROWS, (g + 1) * ROWS)
            dq_out[0, :, lanes((x * per + h * GROUP + g) * DH, DH)] = (
                dq_t[h, :, own].T * SCALE
            ).astype(BF16)

    for step in range(n_z, 2 * n_z - 5):
        hops(0, step, 2)

    kv_width = KVH * DH

    def finish(h):
        for way in range(2):
            @pl.when(z > 0 if way == 0 else z < n_z - 1)
            def _(way=way):
                d_copy(h, z, way).wait_recv()
        for w in range(2):
            def total(rows):
                acc = d_send[h, z, w, rows, :].astype(F32)
                for way in range(2):
                    acc = acc + d_recv[h, way, z, w, rows, :].astype(F32)
                return acc.astype(BF16)

            kx_send[h, w] = total(row_half(other))
            kv_out[0, :, lanes(w * kv_width + (MINE * x + h) * DH, DH)] = total(row_half(x))
        start(send(kx_send.at[h], kx_recv.at[h], kx_s.at[h], kx_r.at[h], ctx=nbr))

    hops(1, 0, 1)
    finish(0)
    for step in range(1, n_z - 2):
        hops(1, step, 1)
    finish(1)
    for h in range(MINE):
        send(kx_send.at[h], kx_recv.at[h], kx_s.at[h], kx_r.at[h], ctx=nbr).wait_recv()
        for w in range(2):
            kv_out[0, :, lanes(w * kv_width + (MINE * other + h) * DH, DH)] = kx_recv[h, w]

    kv_low = kv_out[0]
    mixed_up = dot_nt(adapter_low[:, D:], kv_low).astype(BF16)
    grad = jnp.concatenate([dot_nn(mixed_up, hid_v[...]), dot_nn(mixed_down, kv_low)], axis=1)

    def folded(block):
        return jnp.concatenate([block[:, :fold], block[:, fold:]], axis=0).astype(BF16)

    for d in range(n_dp):
        g_send[d] = folded(grad[:, d * width : (d + 1) * width])
    for step in range(1, n_dp):
        peer = lax.rem(me_dp + step, n_dp)
        start(send(g_send.at[peer], g_recv.at[me_dp], g_s.at[step], g_r.at[me_dp], dp=peer))
    g_recv[me_dp] = g_send[me_dp]

    for h in range(MINE):
        send(dq_send.at[h], dq_recv.at[h], dq_s.at[h], dq_r.at[h], ctx=nbr).wait_recv()
        dq_out[0, :, lanes((MINE * other + h) * heads, heads)] = dq_recv[h]

    for step in range(1, n_dp):
        src = lax.rem(me_dp + step, n_dp)
        send(g_send.at[src], g_recv.at[src], g_s.at[step], g_r.at[src], dp=src).wait_recv()
    part = g_recv[0].astype(F32)
    for d in range(1, n_dp):
        part = part + g_recv[d].astype(F32)
    c_recv[me] = part.astype(BF16)
    for step in range(1, n_ctx):
        peer = lax.rem(me + step, n_ctx)
        start(send(c_recv.at[me], c_recv.at[me], c_s.at[step], c_r.at[me], ctx=peer))
    for step in range(1, n_ctx):
        src = lax.rem(me + step, n_ctx)
        send(c_recv.at[src], c_recv.at[src], c_s.at[step], c_r.at[src], ctx=src).wait_recv()
    whole = c_recv[0].astype(F32)
    for c in range(1, n_ctx):
        whole = whole + c_recv[c].astype(F32)
    grad_own = jnp.concatenate([whole[: whole.shape[0] // 2], whole[whole.shape[0] // 2 :]], axis=1)
    squares = jnp.sum(grad_own * grad_own, axis=(0, 1), keepdims=True)
    sq_recv[me_dp] = jnp.broadcast_to(squares, sq_recv.shape[1:])
    for step in range(1, n_dp):
        peer = lax.rem(me_dp + step, n_dp)
        start(send(sq_recv.at[me_dp], sq_recv.at[me_dp], sq_s.at[step], sq_r.at[me_dp], dp=peer))
    for step in range(1, n_dp):
        src = lax.rem(me_dp + step, n_dp)
        send(sq_recv.at[src], sq_recv.at[src], sq_s.at[step], sq_r.at[src], dp=src).wait_recv()
    total_sq = sq_recv[0]
    for d in range(1, n_dp):
        total_sq = total_sq + sq_recv[d]
    clip = jnp.minimum(1.0, 1.0 / jnp.sqrt(total_sq + 1e-06))[0:1, 0:1]
    scaled = grad_own * clip
    moment = 0.9 * m1_v[...] + 0.1 * scaled
    second = 0.999 * m2_v[...] + 0.001 * scaled * scaled
    step_out[...] = moment / BIAS_ONE / (jnp.sqrt(second / BIAS_TWO) + 1e-08)

    for copy in sends:
        copy.wait_send()
    for h in range(MINE):
        for dest in range(n_z):
            for way in range(2):
                @pl.when((dest > z if way == 0 else dest < z))
                def _(dest=dest, way=way):
                    d_copy(h, dest, way).wait_send()

                @pl.when((dest <= z if way == 0 else dest >= z) & has_next(way))
                def _(dest=dest, way=way):
                    for part in range(2):
                        z_copy(h, part, dest, way).wait_send()


def per_device(n_dp, n_ctx, *args):
    args = list(args)
    args[7] = jnp.swapaxes(args[7], 1, 2)
    adapter = args[8]
    rank, width = adapter.shape
    n_z = n_ctx // 2
    hbm = pl.BlockSpec(memory_space=pl.ANY)
    heads = GROUP * DH
    stack = 2 * GROUP * ROWS
    dma = pltpu.SemaphoreType.DMA
    vmem = pl.BlockSpec(memory_space=pltpu.VMEM)
    fold = (2 * rank, width // 2)
    return pl.pallas_call(
        functools.partial(kernel, n_dp, n_ctx),
        out_shape=(
            jax.ShapeDtypeStruct((1, ROWS, H * DH), BF16),
            jax.ShapeDtypeStruct((1, ROWS, 2 * KVH * DH), BF16),
            jax.ShapeDtypeStruct((rank, width), F32),
        ),
        in_specs=[pl.BlockSpec(memory_space=pltpu.SMEM)] + [hbm] * 10,
        out_specs=(vmem, vmem, vmem),
        scratch_shapes=[
            pltpu.VMEM((MINE, n_z, 2, 2 * ROWS, DH), BF16),
            pltpu.VMEM((2, H, ROWS), F32),
            pltpu.VMEM((H, ROWS), F32),
            pltpu.VMEM((MINE, stack, DH), BF16),
            pltpu.VMEM((MINE, stack, DH), BF16),
            pltpu.VMEM((MINE, 1, stack), F32),
            pltpu.VMEM((MINE, 1, stack), F32),
            pltpu.VMEM((MINE, DH, stack), F32),
            pltpu.VMEM((MINE, n_z, 2, 2 * ROWS, DH), BF16),
            pltpu.VMEM((MINE, 2, n_z, 2, 2 * ROWS, DH), BF16),
            pltpu.VMEM((MINE, ROWS, heads), BF16),
            pltpu.VMEM((MINE, ROWS, heads), BF16),
            pltpu.VMEM((MINE, 2, ROWS, DH), BF16),
            pltpu.VMEM((MINE, 2, ROWS, DH), BF16),
            pltpu.VMEM((n_dp, rank, width), F32),
            pltpu.VMEM((n_dp,) + fold, BF16),
            pltpu.VMEM((n_dp,) + fold, BF16),
            pltpu.VMEM((n_ctx,) + fold, BF16),
            pltpu.VMEM((n_dp, 8, 128), F32),
            pltpu.VMEM((ROWS, D), BF16),
            pltpu.VMEM((ROWS, H * DH), BF16),
            pltpu.VMEM((ROWS, H * DH), BF16),
            pltpu.VMEM((H, ROWS), F32),
            pltpu.VMEM((rank, width), F32),
            pltpu.VMEM((rank, width), F32),
            dma((MINE, 2)), dma((MINE, 2)),
            dma((MINE, 2, GROUP)), dma((MINE, 2, GROUP)),
            dma((1,)), dma((1,)),
            dma((MINE, 2, 2, n_z)), dma((MINE, 2, n_z)),
            dma((MINE, n_z)), dma((MINE, 2, n_z)),
            dma((MINE,)), dma((MINE,)),
            dma((MINE,)), dma((MINE,)),
            dma((n_dp,)), dma((n_dp,)),
            dma((n_dp,)), dma((n_dp,)),
            dma((n_ctx,)), dma((n_ctx,)),
            dma((n_dp,)), dma((n_dp,)),
            dma((MINE, 2)), dma((MINE, 2, GROUP)), dma((7,)),
        ],
        compiler_params=pltpu.CompilerParams(
            collective_id=0, has_side_effects=True, vmem_limit_bytes=60 * 2**20
        ),
        cost_estimate=pl.CostEstimate(flops=3 * 10**9, bytes_accessed=4 * 2**20, transcendentals=2**21),
    )(*args)


def solution(mesh):
    rows = P("dp", "ctx", None)
    columns = P(None, "dp")
    return jax.shard_map(
        functools.partial(per_device, mesh.shape["dp"], mesh.shape["ctx"]),
        mesh=mesh,
        in_specs=(P("dp", None),) + (rows,) * 7 + (columns,) * 3,
        out_specs=(rows, rows, columns),
        check_vma=False,
    )
```

```python
import functools

import jax
import jax.numpy as jnp
from jax import lax
from jax.experimental import pallas as pl
from jax.experimental.pallas import tpu as pltpu
from jax.sharding import PartitionSpec as P

D = 4096
H = 16
KVH = 4
DH = 128
ROWS = 128
HALF = 64
GROUP = H // KVH
MINE = KVH // 2
CHUNK = 2 * ROWS
SCALE = DH ** (-0.5)
BIAS_ONE = 1.0 - 0.9**100.0
BIAS_TWO = 1.0 - 0.999**100.0
F32 = jnp.float32
BF16 = jnp.bfloat16


def dot_nn(a, b):
    return jnp.dot(a, b, preferred_element_type=F32)


def dot_nt(a, b):
    return lax.dot_general(a, b, (((1,), (1,)), ((), ())), preferred_element_type=F32)


def dot_tn(a, b):
    return lax.dot_general(a, b, (((0,), (0,)), ((), ())), preferred_element_type=F32)


def lanes(start, width):
    return pl.ds(pl.multiple_of(start, DH), width)


def send(src, dst, send_sem, recv_sem, **target):
    return pltpu.make_async_remote_copy(
        src_ref=src,
        dst_ref=dst,
        send_sem=send_sem,
        recv_sem=recv_sem,
        device_id=target,
        device_id_type=pl.DeviceIdType.MESH,
    )


def kernel(
    n_dp, n_ctx,
    span_ref, hid_ref, q_ref, k_ref, v_ref, o_ref, do_ref, ln_ref, ad_ref, m1_ref, m2_ref,
    dq_out, kv_out, step_out,
    kv_all, stat, stat_nbr, q_st, do_st, ln_row, de_row, dq_t, d_early,
    d_send, d_recv, dq_send, dq_recv, kx_send, kx_recv,
    ad_all, g_send, g_recv, c_recv, sq_recv,
    hid_v, o_v, do_v, ln_v, m1_v, m2_v,
    xk_s, xk_r, xq_s, xq_r, st_s, st_r, z_s, z_r, d_s, d_r, dq_s, dq_r, kx_s, kx_r,
    ad_s, ad_r, g_s, g_r, c_s, c_r, sq_s, sq_r, l_kv, l_q, l_s,
):
    me_dp = lax.axis_index("dp")
    me = lax.axis_index("ctx")
    n_z = n_ctx // 2
    z, x = me // 2, lax.rem(me, 2)
    other = 1 - x
    nbr = 2 * z + other
    width = ad_ref.shape[1]
    fold = width // 2
    per = H // 2
    heads = GROUP * DH
    sources = (k_ref, v_ref)
    sends = []

    def start(copy):
        copy.start()
        sends.append(copy)

    def row_half(part):
        return pl.ds(pl.multiple_of(part * ROWS, ROWS), ROWS)

    own_kv = [
        [
            pltpu.make_async_copy(
                sources[w].at[0, :, lanes((MINE * x + h) * DH, DH)],
                kv_all.at[h, z, w, row_half(x), :],
                l_kv.at[h, w],
            )
            for w in range(2)
        ]
        for h in range(MINE)
    ]
    own_q = [
        pltpu.make_async_copy(
            src.at[0, :, lanes((x * per + h * GROUP + g) * DH, DH)],
            dst.at[h, g * ROWS : (g + 1) * ROWS, :],
            l_q.at[h, w, g],
        )
        for h in range(MINE)
        for w, (src, dst) in enumerate(((q_ref, q_st), (do_ref, do_st)))
        for g in range(GROUP)
    ]
    own_rest = [
        pltpu.make_async_copy(src, dst, l_s.at[i])
        for i, (src, dst) in enumerate((
            (do_ref.at[0], do_v), (o_ref.at[0], o_v), (ln_ref.at[0], ln_v),
            (ad_ref, ad_all.at[me_dp]), (hid_ref.at[0], hid_v), (m1_ref, m1_v), (m2_ref, m2_v),
        ))
    ]
    for copy in own_kv[0] + own_kv[1] + own_rest[:4] + own_q + own_rest[4:]:
        copy.start()

    barrier = pltpu.get_barrier_semaphore()
    for step in range(1, n_ctx):
        pl.semaphore_signal(barrier, inc=1, device_id={"ctx": lax.rem(me + step, n_ctx)},
                            device_id_type=pl.DeviceIdType.MESH)
    for step in range(1, n_dp):
        pl.semaphore_signal(barrier, inc=1, device_id={"dp": lax.rem(me_dp + step, n_dp)},
                            device_id_type=pl.DeviceIdType.MESH)
    for copy in own_rest[:4]:
        copy.wait()
    for part in range(2):
        stat[part, 0:per, :] = ln_v[part * per : (part + 1) * per, :]
    for head in range(H):
        cols = slice(head * DH, (head + 1) * DH)
        prod = do_v[:, cols].astype(F32) * o_v[:, cols].astype(F32)
        at = per + head % per
        stat[head // per, at : at + 1, :] = jnp.sum(prod.T, axis=0, keepdims=True)
    pl.semaphore_wait(barrier, n_ctx - 1 + n_dp - 1)

    def x_kv(h, w, part):
        return send(
            sources[w].at[0, :, lanes((MINE * other + h) * DH, DH)],
            kv_all.at[h, z, w, row_half(part), :],
            xk_s.at[h, w], xk_r.at[h, w], ctx=nbr,
        )

    def x_q(h, w, g):
        src, dst = ((q_ref, q_st), (do_ref, do_st))[w]
        return send(
            src.at[0, :, lanes((other * per + h * GROUP + g) * DH, DH)],
            dst.at[h, (GROUP + g) * ROWS : (GROUP + g + 1) * ROWS, :],
            xq_s.at[h, w, g], xq_r.at[h, w, g], ctx=nbr,
        )

    def next_z(way):
        return z + 1 if way == 0 else z - 1

    def has_next(way):
        return z < n_z - 1 if way == 0 else z > 0

    def z_copy(h, part, owner, way):
        rows = row_half(x if part == 0 else other)
        return send(
            kv_all.at[h, owner, :, rows, :], kv_all.at[h, owner, :, rows, :],
            z_s.at[h, part, way, owner], z_r.at[h, part, owner], ctx=2 * next_z(way) + x,
        )

    def z_push(h, part):
        for way in range(2):
            @pl.when(has_next(way))
            def _(way=way):
                z_copy(h, part, z, way).start()

    def relay_block(h, owner, way):
        for part in range(2):
            z_copy(h, part, owner, way).wait_recv()

            @pl.when(has_next(way))
            def _(part=part):
                z_copy(h, part, owner, way).start()

    def z_relay(h, distance):
        for way in range(2):
            owner = z - distance if way == 0 else z + distance

            @pl.when((owner >= 0) & (owner < n_z))
            def _(way=way, owner=owner):
                relay_block(h, owner, way)

    for h in range(MINE):
        for w in range(2):
            start(x_kv(h, w, x))
    for copy in own_kv[0]:
        copy.wait()
    z_push(0, 0)
    for w in range(2):
        for g in range(GROUP):
            start(x_q(0, w, g))
    for step in range(1, n_dp):
        peer = lax.rem(me_dp + step, n_dp)
        start(send(ad_ref, ad_all.at[me_dp], ad_s.at[step], ad_r.at[me_dp], dp=peer))

    start(send(stat.at[other], stat_nbr, st_s.at[0], st_r.at[0], ctx=nbr))
    for w in range(2):
        for g in range(GROUP):
            start(x_q(1, w, g))
    for w in range(2):
        x_kv(0, w, other).wait_recv()
    z_push(0, 1)

    @pl.when(z == 0)
    def _():
        for h in range(MINE):
            d_recv[h, 0, z] = jnp.zeros(d_recv.shape[3:], BF16)

    @pl.when(z == n_z - 1)
    def _():
        for h in range(MINE):
            d_recv[h, 1, z] = jnp.zeros(d_recv.shape[3:], BF16)

    for copy in own_kv[1] + own_q:
        copy.wait()
    def rows_of(src, at_group):
        for h in range(MINE):
            for g in range(GROUP):
                at = h * GROUP + g
                cols = slice((at_group + g) * ROWS, (at_group + g + 1) * ROWS)
                ln_row[h, :, cols] = src(at)
                de_row[h, :, cols] = src(per + at)

    rows_of(lambda at: stat[x, at : at + 1, :], 0)
    lane_row = lax.rem(lax.broadcasted_iota(jnp.int32, (1, CHUNK), 1), ROWS)
    key_row = lax.broadcasted_iota(jnp.int32, (2 * ROWS, 1), 0)

    def query_pos(device):
        first, second = span_ref[0, 2 * device], span_ref[0, 2 * device + 1]
        return jnp.where(lane_row < HALF, first * HALF + lane_row, second * HALF + lane_row - HALF)

    pos_own, pos_far = query_pos(me), query_pos(nbr)
    chunks = 2 * GROUP * ROWS // CHUNK

    def d_copy(h, dest, way):
        return send(d_send.at[h, dest], d_recv.at[h, way, dest], d_s.at[h, dest],
                    d_r.at[h, way, dest], ctx=2 * next_z(way) + x)

    def hops(h, step, lag):
        for way in range(2):
            before = z if way == 0 else n_z - 1 - z
            turn = step - lag * (before - 1)
            dest = n_z - 1 - turn if way == 0 else turn
            ahead = dest > z if way == 0 else dest < z

            @pl.when((before > 0) & (turn >= 0) & ahead)
            def _(way=way, dest=dest):
                d_copy(h, dest, way).wait_recv()
                both = d_send[h, dest].astype(F32) + d_recv[h, way, dest].astype(F32)
                d_send[h, dest] = both.astype(BF16)
                d_copy(h, dest, way).start()

    def terms(h, t, parts):
        keys, values = kv_all[h, t, 0], kv_all[h, t, 1]
        pos_key = jnp.zeros_like(key_row)
        for s in range(4):
            base = (span_ref[0, 4 * t + s] - s) * HALF
            pos_key = jnp.where(key_row // HALF == s, base + key_row, pos_key)
        dk = jnp.zeros((2 * ROWS, DH), F32)
        dv = jnp.zeros((2 * ROWS, DH), F32)
        for j in parts:
            cols = slice(j * CHUNK, (j + 1) * CHUNK)
            q_rows, do_rows = q_st[h, cols, :], do_st[h, cols, :]
            scores = dot_nt(keys, q_rows) * SCALE
            visible = pos_key <= (pos_own if j < chunks // 2 else pos_far)
            weights = jnp.where(visible, jnp.exp(scores - ln_row[h, :, cols]), 0.0)
            d_weights = dot_nt(values, do_rows)
            d_scores = (weights * (d_weights - de_row[h, :, cols])).astype(BF16)
            dv = dv + dot_nn(weights.astype(BF16), do_rows)
            dk = dk + dot_nn(d_scores, q_rows)
            dq_t[h, :, cols] += dot_tn(keys, d_scores)
        return dk, dv

    for h in range(MINE):
        dq_t[h] = jnp.zeros(dq_t.shape[1:], F32)

    def early(index, carry):
        distance, way = (index + 1) // 2, lax.rem(index + 1, 2)
        owner = jnp.where(way == 0, z - distance, z + distance)

        @pl.when((owner >= 0) & (owner < n_z))
        def _():
            for which in range(2):
                @pl.when((way == which) & (distance > 0))
                def _(which=which):
                    relay_block(0, owner, which)

            dk, dv = terms(0, owner, range(chunks // 2))
            d_early[owner, 0] = dk
            d_early[owner, 1] = dv

        @pl.when(index == 2 * (n_z - 2))
        def _():
            z_push(1, 0)
            for w in range(2):
                x_kv(1, w, other).wait_recv()
            z_push(1, 1)

        return carry

    lax.fori_loop(0, 2 * n_z - 1, early, 0)

    for copy in own_rest[4:]:
        copy.wait()
    for step in range(1, n_dp):
        src = lax.rem(me_dp + step, n_dp)
        send(ad_ref, ad_all.at[src], ad_s.at[step], ad_r.at[src], dp=src).wait_recv()
    adapter_low = jnp.concatenate([ad_all[d] for d in range(n_dp)], axis=1).astype(BF16)
    mixed_down = dot_nt(adapter_low[:, :D], hid_v[...]).astype(BF16)

    send(stat.at[other], stat_nbr, st_s.at[0], st_r.at[0], ctx=nbr).wait_recv()
    rows_of(lambda at: stat_nbr[at : at + 1, :], GROUP)

    def dq_finish(h):
        for g in range(GROUP):
            far = slice((GROUP + g) * ROWS, (GROUP + g + 1) * ROWS)
            dq_send[h, :, g * DH : (g + 1) * DH] = (dq_t[h, :, far].T * SCALE).astype(BF16)
        start(send(dq_send.at[h], dq_recv.at[h], dq_s.at[h], dq_r.at[h], ctx=nbr))
        for g in range(GROUP):
            own = slice(g * ROWS, (g + 1) * ROWS)
            dq_out[0, :, lanes((x * per + h * GROUP + g) * DH, DH)] = (
                dq_t[h, :, own].T * SCALE
            ).astype(BF16)

    for h in range(MINE):
        for w in range(2):
            for g in range(GROUP):
                x_q(h, w, g).wait_recv()

        def block(step, carry, h=h):
            t = jnp.where(lax.rem(step, 2) == 0, n_z - 1 - step // 2, step // 2)
            if h == 0:
                dk, dv = terms(h, t, range(chunks // 2, chunks))
                dk, dv = dk + d_early[t, 0], dv + d_early[t, 1]
            else:
                dk, dv = terms(h, t, range(chunks))
            d_send[h, t, 0] = (dk * SCALE).astype(BF16)
            d_send[h, t, 1] = dv.astype(BF16)

            @pl.when((z == 0) & (t > z))
            def _():
                d_copy(h, t, 0).start()

            @pl.when((z == n_z - 1) & (t < z))
            def _():
                d_copy(h, t, 1).start()

            if h == 0:
                @pl.when(step > 0)
                def _():
                    z_relay(1, step)
            else:
                hops(0, step, 2)

                @pl.when((step > 0) & (lax.rem(step, 2) == 0))
                def _():
                    hops(1, step // 2 - 1, 1)

            return carry

        lax.fori_loop(0, n_z, block, 0)
        if h == 0:
            dq_finish(0)

    for step in range(n_z, 2 * n_z - 5):
        hops(0, step, 2)

    kv_width = KVH * DH

    def finish(h):
        for way in range(2):
            @pl.when(z > 0 if way == 0 else z < n_z - 1)
            def _(way=way):
                d_copy(h, z, way).wait_recv()
        for w in range(2):
            def total(rows):
                acc = d_send[h, z, w, rows, :].astype(F32)
                for way in range(2):
                    acc = acc + d_recv[h, way, z, w, rows, :].astype(F32)
                return acc.astype(BF16)

            kx_send[h, w] = total(row_half(other))
            kv_out[0, :, lanes(w * kv_width + (MINE * x + h) * DH, DH)] = total(row_half(x))
        start(send(kx_send.at[h], kx_recv.at[h], kx_s.at[h], kx_r.at[h], ctx=nbr))

    done = (n_z + 1) // 2 - 1
    for step in range(done, n_z - 2):
        hops(1, step, 1)
    finish(0)
    dq_finish(1)
    finish(1)
    for h in range(MINE):
        send(kx_send.at[h], kx_recv.at[h], kx_s.at[h], kx_r.at[h], ctx=nbr).wait_recv()
        for w in range(2):
            kv_out[0, :, lanes(w * kv_width + (MINE * other + h) * DH, DH)] = kx_recv[h, w]

    kv_low = kv_out[0]
    mixed_up = dot_nt(adapter_low[:, D:], kv_low).astype(BF16)
    grad = jnp.concatenate([dot_nn(mixed_up, hid_v[...]), dot_nn(mixed_down, kv_low)], axis=1)

    def folded(block):
        return jnp.concatenate([block[:, :fold], block[:, fold:]], axis=0).astype(BF16)

    for d in range(n_dp):
        g_send[d] = folded(grad[:, d * width : (d + 1) * width])
    for step in range(1, n_dp):
        peer = lax.rem(me_dp + step, n_dp)
        start(send(g_send.at[peer], g_recv.at[me_dp], g_s.at[step], g_r.at[me_dp], dp=peer))
    g_recv[me_dp] = g_send[me_dp]

    for h in range(MINE):
        send(dq_send.at[h], dq_recv.at[h], dq_s.at[h], dq_r.at[h], ctx=nbr).wait_recv()
        dq_out[0, :, lanes((MINE * other + h) * heads, heads)] = dq_recv[h]

    for step in range(1, n_dp):
        src = lax.rem(me_dp + step, n_dp)
        send(g_send.at[src], g_recv.at[src], g_s.at[step], g_r.at[src], dp=src).wait_recv()
    part = g_recv[0].astype(F32)
    for d in range(1, n_dp):
        part = part + g_recv[d].astype(F32)
    c_recv[me] = part.astype(BF16)
    for step in range(1, n_ctx):
        peer = lax.rem(me + step, n_ctx)
        start(send(c_recv.at[me], c_recv.at[me], c_s.at[step], c_r.at[me], ctx=peer))
    for step in range(1, n_ctx):
        src = lax.rem(me + step, n_ctx)
        send(c_recv.at[src], c_recv.at[src], c_s.at[step], c_r.at[src], ctx=src).wait_recv()
    whole = c_recv[0].astype(F32)
    for c in range(1, n_ctx):
        whole = whole + c_recv[c].astype(F32)
    grad_own = jnp.concatenate([whole[: whole.shape[0] // 2], whole[whole.shape[0] // 2 :]], axis=1)
    squares = jnp.sum(grad_own * grad_own, axis=(0, 1), keepdims=True)
    sq_recv[me_dp] = jnp.broadcast_to(squares, sq_recv.shape[1:])
    for step in range(1, n_dp):
        peer = lax.rem(me_dp + step, n_dp)
        start(send(sq_recv.at[me_dp], sq_recv.at[me_dp], sq_s.at[step], sq_r.at[me_dp], dp=peer))
    for step in range(1, n_dp):
        src = lax.rem(me_dp + step, n_dp)
        send(sq_recv.at[src], sq_recv.at[src], sq_s.at[step], sq_r.at[src], dp=src).wait_recv()
    total_sq = sq_recv[0]
    for d in range(1, n_dp):
        total_sq = total_sq + sq_recv[d]
    clip = jnp.minimum(1.0, 1.0 / jnp.sqrt(total_sq + 1e-06))[0:1, 0:1]
    scaled = grad_own * clip
    moment = 0.9 * m1_v[...] + 0.1 * scaled
    second = 0.999 * m2_v[...] + 0.001 * scaled * scaled
    step_out[...] = moment / BIAS_ONE / (jnp.sqrt(second / BIAS_TWO) + 1e-08)

    for copy in sends:
        copy.wait_send()
    for h in range(MINE):
        for dest in range(n_z):
            for way in range(2):
                @pl.when((dest > z if way == 0 else dest < z))
                def _(dest=dest, way=way):
                    d_copy(h, dest, way).wait_send()

                @pl.when((dest <= z if way == 0 else dest >= z) & has_next(way))
                def _(dest=dest, way=way):
                    for part in range(2):
                        z_copy(h, part, dest, way).wait_send()


def per_device(n_dp, n_ctx, *args):
    args = list(args)
    args[7] = jnp.swapaxes(args[7], 1, 2)
    adapter = args[8]
    rank, width = adapter.shape
    n_z = n_ctx // 2
    hbm = pl.BlockSpec(memory_space=pltpu.HBM)
    heads = GROUP * DH
    stack = 2 * GROUP * ROWS
    dma = pltpu.SemaphoreType.DMA
    vmem = pl.BlockSpec(memory_space=pltpu.VMEM)
    fold = (2 * rank, width // 2)
    return pl.pallas_call(
        functools.partial(kernel, n_dp, n_ctx),
        out_shape=(
            jax.ShapeDtypeStruct((1, ROWS, H * DH), BF16),
            jax.ShapeDtypeStruct((1, ROWS, 2 * KVH * DH), BF16),
            jax.ShapeDtypeStruct((rank, width), F32),
        ),
        in_specs=[pl.BlockSpec(memory_space=pltpu.SMEM)] + [hbm] * 10,
        out_specs=(vmem, vmem, vmem),
        scratch_shapes=[
            pltpu.VMEM((MINE, n_z, 2, 2 * ROWS, DH), BF16),
            pltpu.VMEM((2, H, ROWS), F32),
            pltpu.VMEM((H, ROWS), F32),
            pltpu.VMEM((MINE, stack, DH), BF16),
            pltpu.VMEM((MINE, stack, DH), BF16),
            pltpu.VMEM((MINE, 1, stack), F32),
            pltpu.VMEM((MINE, 1, stack), F32),
            pltpu.VMEM((MINE, DH, stack), F32),
            pltpu.VMEM((n_z, 2, 2 * ROWS, DH), F32),
            pltpu.VMEM((MINE, n_z, 2, 2 * ROWS, DH), BF16),
            pltpu.VMEM((MINE, 2, n_z, 2, 2 * ROWS, DH), BF16),
            pltpu.VMEM((MINE, ROWS, heads), BF16),
            pltpu.VMEM((MINE, ROWS, heads), BF16),
            pltpu.VMEM((MINE, 2, ROWS, DH), BF16),
            pltpu.VMEM((MINE, 2, ROWS, DH), BF16),
            pltpu.VMEM((n_dp, rank, width), F32),
            pltpu.VMEM((n_dp,) + fold, BF16),
            pltpu.VMEM((n_dp,) + fold, BF16),
            pltpu.VMEM((n_ctx,) + fold, BF16),
            pltpu.VMEM((n_dp, 8, 128), F32),
            pltpu.VMEM((ROWS, D), BF16),
            pltpu.VMEM((ROWS, H * DH), BF16),
            pltpu.VMEM((ROWS, H * DH), BF16),
            pltpu.VMEM((H, ROWS), F32),
            pltpu.VMEM((rank, width), F32),
            pltpu.VMEM((rank, width), F32),
            dma((MINE, 2)), dma((MINE, 2)),
            dma((MINE, 2, GROUP)), dma((MINE, 2, GROUP)),
            dma((1,)), dma((1,)),
            dma((MINE, 2, 2, n_z)), dma((MINE, 2, n_z)),
            dma((MINE, n_z)), dma((MINE, 2, n_z)),
            dma((MINE,)), dma((MINE,)),
            dma((MINE,)), dma((MINE,)),
            dma((n_dp,)), dma((n_dp,)),
            dma((n_dp,)), dma((n_dp,)),
            dma((n_ctx,)), dma((n_ctx,)),
            dma((n_dp,)), dma((n_dp,)),
            dma((MINE, 2)), dma((MINE, 2, GROUP)), dma((7,)),
        ],
        compiler_params=pltpu.CompilerParams(
            collective_id=0, has_side_effects=True, vmem_limit_bytes=40 * 2**20
        ),
        cost_estimate=pl.CostEstimate(flops=3 * 10**9, bytes_accessed=4 * 2**20, transcendentals=2**21),
    )(*args)


def solution(mesh):
    rows = P("dp", "ctx", None)
    columns = P(None, "dp")
    return jax.shard_map(
        functools.partial(per_device, mesh.shape["dp"], mesh.shape["ctx"]),
        mesh=mesh,
        in_specs=(P("dp", None),) + (rows,) * 7 + (columns,) * 3,
        out_specs=(rows, rows, columns),
        check_vma=False,
    )
```

```python
import functools

import jax
import jax.numpy as jnp
from jax import lax
from jax.experimental import pallas as pl
from jax.experimental.pallas import tpu as pltpu
from jax.sharding import PartitionSpec as P

D = 4096
H = 16
KVH = 4
DH = 128
ROWS = 128
HALF = 64
GROUP = H // KVH
MINE = KVH // 2
CHUNK = 2 * ROWS
SCALE = DH ** (-0.5)
LOG2E = 1.4426950408889634
BIAS_ONE = 1.0 - 0.9**100.0
BIAS_TWO = 1.0 - 0.999**100.0
F32 = jnp.float32
BF16 = jnp.bfloat16


def dot_nn(a, b):
    return jnp.dot(a, b, preferred_element_type=F32)


def dot_nt(a, b):
    return lax.dot_general(a, b, (((1,), (1,)), ((), ())), preferred_element_type=F32)


def dot_tn(a, b):
    return lax.dot_general(a, b, (((0,), (0,)), ((), ())), preferred_element_type=F32)


def lanes(start, width):
    return pl.ds(pl.multiple_of(start, DH), width)


def send(src, dst, send_sem, recv_sem, **target):
    return pltpu.make_async_remote_copy(
        src_ref=src,
        dst_ref=dst,
        send_sem=send_sem,
        recv_sem=recv_sem,
        device_id=target,
        device_id_type=pl.DeviceIdType.MESH,
    )


def kernel(
    n_dp, n_ctx,
    span_ref, hid_ref, q_ref, k_ref, v_ref, o_ref, do_ref, ln_ref, ad_ref, m1_ref, m2_ref,
    dq_out, kv_out, step_out,
    kv_all, stat, stat_nbr, q_st, do_st, ln_row, de_row, dq_t,
    d_send, d_recv, dq_send, dq_recv, kx_send, kx_recv,
    ad_all, g_send, g_recv, c_recv, sq_recv,
    hid_v, o_v, do_v, ln_v, m1_v, m2_v,
    xk_s, xk_r, xq_s, xq_r, st_s, st_r, z_s, z_r, d_s, d_r, dq_s, dq_r, kx_s, kx_r,
    ad_s, ad_r, g_s, g_r, c_s, c_r, sq_s, sq_r, l_kv, l_q, l_s,
):
    me_dp = lax.axis_index("dp")
    me = lax.axis_index("ctx")
    n_z = n_ctx // 2
    z, x = me // 2, lax.rem(me, 2)
    other = 1 - x
    nbr = 2 * z + other
    width = ad_ref.shape[1]
    fold = width // 2
    per = H // 2
    heads = GROUP * DH
    sources = (k_ref, v_ref)
    sends = []

    def start(copy):
        copy.start()
        sends.append(copy)

    def row_half(part):
        return pl.ds(pl.multiple_of(part * ROWS, ROWS), ROWS)

    own_kv = [
        [
            pltpu.make_async_copy(
                sources[w].at[0, :, lanes((MINE * x + h) * DH, DH)],
                kv_all.at[h, z, w, row_half(x), :],
                l_kv.at[h, w],
            )
            for w in range(2)
        ]
        for h in range(MINE)
    ]
    own_q = [
        pltpu.make_async_copy(
            src.at[0, :, lanes((x * per + h * GROUP + g) * DH, DH)],
            dst.at[h, g * ROWS : (g + 1) * ROWS, :],
            l_q.at[h, w, g],
        )
        for h in range(MINE)
        for w, (src, dst) in enumerate(((q_ref, q_st), (do_ref, do_st)))
        for g in range(GROUP)
    ]
    own_rest = [
        pltpu.make_async_copy(src, dst, l_s.at[i])
        for i, (src, dst) in enumerate((
            (do_ref.at[0], do_v), (o_ref.at[0], o_v), (ln_ref.at[0], ln_v),
            (ad_ref, ad_all.at[me_dp]), (hid_ref.at[0], hid_v), (m1_ref, m1_v), (m2_ref, m2_v),
        ))
    ]
    for copy in own_kv[0] + own_kv[1] + own_rest[:4] + own_q + own_rest[4:]:
        copy.start()

    barrier = pltpu.get_barrier_semaphore()
    for step in range(1, n_ctx):
        pl.semaphore_signal(barrier, inc=1, device_id={"ctx": lax.rem(me + step, n_ctx)},
                            device_id_type=pl.DeviceIdType.MESH)
    for step in range(1, n_dp):
        pl.semaphore_signal(barrier, inc=1, device_id={"dp": lax.rem(me_dp + step, n_dp)},
                            device_id_type=pl.DeviceIdType.MESH)
    for copy in own_rest[:4]:
        copy.wait()
    for part in range(2):
        stat[part, 0:per, :] = ln_v[part * per : (part + 1) * per, :]
    for head in range(H):
        cols = slice(head * DH, (head + 1) * DH)
        prod = do_v[:, cols].astype(F32) * o_v[:, cols].astype(F32)
        at = per + head % per
        stat[head // per, at : at + 1, :] = jnp.sum(prod.T, axis=0, keepdims=True)
    pl.semaphore_wait(barrier, n_ctx - 1 + n_dp - 1)

    def x_kv(h, w, part):
        return send(
            sources[w].at[0, :, lanes((MINE * other + h) * DH, DH)],
            kv_all.at[h, z, w, row_half(part), :],
            xk_s.at[h, w], xk_r.at[h, w], ctx=nbr,
        )

    def x_q(h, w, g):
        src, dst = ((q_ref, q_st), (do_ref, do_st))[w]
        return send(
            src.at[0, :, lanes((other * per + h * GROUP + g) * DH, DH)],
            dst.at[h, (GROUP + g) * ROWS : (GROUP + g + 1) * ROWS, :],
            xq_s.at[h, w, g], xq_r.at[h, w, g], ctx=nbr,
        )

    def next_z(way):
        return z + 1 if way == 0 else z - 1

    def has_next(way):
        return z < n_z - 1 if way == 0 else z > 0

    def z_copy(h, part, owner, way):
        rows = row_half(x if part == 0 else other)
        return send(
            kv_all.at[h, owner, :, rows, :], kv_all.at[h, owner, :, rows, :],
            z_s.at[h, part, way, owner], z_r.at[h, part, owner], ctx=2 * next_z(way) + x,
        )

    def z_push(h, part):
        for way in range(2):
            @pl.when(has_next(way))
            def _(way=way):
                z_copy(h, part, z, way).start()

    def z_relay(h, distance):
        for part in range(2):
            for way in range(2):
                owner = z - distance if way == 0 else z + distance

                @pl.when((owner >= 0) & (owner < n_z))
                def _(part=part, way=way, owner=owner):
                    z_copy(h, part, owner, way).wait_recv()

                    @pl.when(has_next(way))
                    def _():
                        z_copy(h, part, owner, way).start()

    for h in range(MINE):
        for w in range(2):
            start(x_kv(h, w, x))
    for copy in own_kv[0]:
        copy.wait()
    z_push(0, 0)
    for w in range(2):
        for g in range(GROUP):
            start(x_q(0, w, g))
    for step in range(1, n_dp):
        peer = lax.rem(me_dp + step, n_dp)
        start(send(ad_ref, ad_all.at[me_dp], ad_s.at[step], ad_r.at[me_dp], dp=peer))

    start(send(stat.at[other], stat_nbr, st_s.at[0], st_r.at[0], ctx=nbr))
    for w in range(2):
        for g in range(GROUP):
            start(x_q(1, w, g))

    for w in range(2):
        x_kv(0, w, other).wait_recv()
    z_push(0, 1)
    for distance in range(1, n_z - 1):
        z_relay(0, distance)
    for copy in own_kv[1]:
        copy.wait()
    z_push(1, 0)
    for w in range(2):
        x_kv(1, w, other).wait_recv()
    z_push(1, 1)

    @pl.when(z == 0)
    def _():
        for h in range(MINE):
            d_recv[h, 0, z] = jnp.zeros(d_recv.shape[3:], BF16)

    @pl.when(z == n_z - 1)
    def _():
        for h in range(MINE):
            d_recv[h, 1, z] = jnp.zeros(d_recv.shape[3:], BF16)

    for copy in own_rest[4:] + own_q:
        copy.wait()
    for step in range(1, n_dp):
        src = lax.rem(me_dp + step, n_dp)
        send(ad_ref, ad_all.at[src], ad_s.at[step], ad_r.at[src], dp=src).wait_recv()
    adapter_low = jnp.concatenate([ad_all[d] for d in range(n_dp)], axis=1).astype(BF16)
    mixed_down = dot_nt(adapter_low[:, :D], hid_v[...]).astype(BF16)

    z_relay(0, n_z - 1)

    send(stat.at[other], stat_nbr, st_s.at[0], st_r.at[0], ctx=nbr).wait_recv()
    for h in range(MINE):
        for g in range(GROUP):
            at = h * GROUP + g
            own = slice(g * ROWS, (g + 1) * ROWS)
            far = slice((GROUP + g) * ROWS, (GROUP + g + 1) * ROWS)
            ln_row[h, :, own] = stat[x, at : at + 1, :] * LOG2E
            ln_row[h, :, far] = stat_nbr[at : at + 1, :] * LOG2E
            de_row[h, :, own] = stat[x, per + at : per + at + 1, :]
            de_row[h, :, far] = stat_nbr[per + at : per + at + 1, :]

    lane_row = lax.broadcasted_iota(jnp.int32, (1, ROWS), 1)
    key_row = lax.broadcasted_iota(jnp.int32, (HALF, ROWS), 0)

    def query_pos(device):
        first, second = span_ref[0, 2 * device], span_ref[0, 2 * device + 1]
        return jnp.where(lane_row < HALF, first * HALF + lane_row, second * HALF + lane_row - HALF)

    pos_own, pos_far = query_pos(me), query_pos(nbr)
    chunks = 2 * GROUP * ROWS // CHUNK

    def d_copy(h, dest, way):
        return send(d_send.at[h, dest], d_recv.at[h, way, dest], d_s.at[h, dest],
                    d_r.at[h, way, dest], ctx=2 * next_z(way) + x)

    def hops(h, step, lag):
        for way in range(2):
            before = z if way == 0 else n_z - 1 - z
            turn = step - lag * (before - 1)
            dest = n_z - 1 - turn if way == 0 else turn
            ahead = dest > z if way == 0 else dest < z

            @pl.when((before > 0) & (turn >= 0) & ahead)
            def _(way=way, dest=dest):
                d_copy(h, dest, way).wait_recv()
                both = d_send[h, dest].astype(F32) + d_recv[h, way, dest].astype(F32)
                d_send[h, dest] = both.astype(BF16)
                d_copy(h, dest, way).start()

    def dq_finish(h):
        for g in range(GROUP):
            far = slice((GROUP + g) * ROWS, (GROUP + g + 1) * ROWS)
            dq_send[h, :, g * DH : (g + 1) * DH] = (dq_t[h, :, far].T * SCALE).astype(BF16)
        start(send(dq_send.at[h], dq_recv.at[h], dq_s.at[h], dq_r.at[h], ctx=nbr))
        for g in range(GROUP):
            own = slice(g * ROWS, (g + 1) * ROWS)
            dq_out[0, :, lanes((x * per + h * GROUP + g) * DH, DH)] = (
                dq_t[h, :, own].T * SCALE
            ).astype(BF16)

    for h in range(MINE):
        for w in range(2):
            for g in range(GROUP):
                x_q(h, w, g).wait_recv()
        dq_t[h] = jnp.zeros(dq_t.shape[1:], F32)

        def block(step, carry, h=h):
            t = jnp.where(lax.rem(step, 2) == 0, n_z - 1 - step // 2, step // 2)
            keys, values = kv_all[h, t, 0], kv_all[h, t, 1]
            keys_t = keys.T
            pos_key = jnp.concatenate(
                [span_ref[0, 4 * t + s] * HALF + key_row for s in range(4)], axis=0
            )
            hidden_from = [
                jnp.where(pos_key <= pos, 0.0, -jnp.inf).astype(F32) for pos in (pos_own, pos_far)
            ]
            dk = jnp.zeros((2 * ROWS, DH), F32)
            dv = jnp.zeros((2 * ROWS, DH), F32)
            for j in range(chunks):
                cols = slice(j * CHUNK, (j + 1) * CHUNK)
                q_rows, do_rows = q_st[h, cols, :], do_st[h, cols, :]
                mask = hidden_from[2 * j // chunks]
                mask = jnp.concatenate([mask] * (CHUNK // ROWS), axis=1)
                scores = dot_nt(keys, q_rows) * (SCALE * LOG2E)
                weights = jnp.exp2(scores - ln_row[h, :, cols] + mask)
                d_weights = dot_nt(values, do_rows)
                d_scores = (weights * (d_weights - de_row[h, :, cols])).astype(BF16)
                dv = dv + dot_nn(weights.astype(BF16), do_rows)
                dk = dk + dot_nn(d_scores, q_rows)
                dq_t[h, :, cols] += dot_nn(keys_t, d_scores)
            d_send[h, t, 0] = (dk * SCALE).astype(BF16)
            d_send[h, t, 1] = dv.astype(BF16)

            @pl.when((z == 0) & (t > z))
            def _():
                d_copy(h, t, 0).start()

            @pl.when((z == n_z - 1) & (t < z))
            def _():
                d_copy(h, t, 1).start()

            if h == 0:
                @pl.when(step > 0)
                def _():
                    z_relay(1, step)
            else:
                hops(0, step, 2)

                @pl.when((step > 0) & (lax.rem(step, 2) == 0))
                def _():
                    hops(1, step // 2 - 1, 1)

            return carry

        lax.fori_loop(0, n_z, block, 0)

        if h == 0:
            dq_finish(0)

    for step in range(n_z, 2 * n_z - 5):
        hops(0, step, 2)

    kv_width = KVH * DH

    def finish(h):
        for way in range(2):
            @pl.when(z > 0 if way == 0 else z < n_z - 1)
            def _(way=way):
                d_copy(h, z, way).wait_recv()
        for w in range(2):
            def total(rows):
                acc = d_send[h, z, w, rows, :].astype(F32)
                for way in range(2):
                    acc = acc + d_recv[h, way, z, w, rows, :].astype(F32)
                return acc.astype(BF16)

            kx_send[h, w] = total(row_half(other))
            kv_out[0, :, lanes(w * kv_width + (MINE * x + h) * DH, DH)] = total(row_half(x))
        start(send(kx_send.at[h], kx_recv.at[h], kx_s.at[h], kx_r.at[h], ctx=nbr))

    for step in range((n_z + 1) // 2 - 1, n_z - 2):
        hops(1, step, 1)
    finish(0)
    dq_finish(1)
    finish(1)
    for h in range(MINE):
        send(kx_send.at[h], kx_recv.at[h], kx_s.at[h], kx_r.at[h], ctx=nbr).wait_recv()
        for w in range(2):
            kv_out[0, :, lanes(w * kv_width + (MINE * other + h) * DH, DH)] = kx_recv[h, w]

    kv_low = kv_out[0]
    mixed_up = dot_nt(adapter_low[:, D:], kv_low).astype(BF16)
    grad = jnp.concatenate([dot_nn(mixed_up, hid_v[...]), dot_nn(mixed_down, kv_low)], axis=1)

    def folded(block):
        return jnp.concatenate([block[:, :fold], block[:, fold:]], axis=0).astype(BF16)

    for d in range(n_dp):
        g_send[d] = folded(grad[:, d * width : (d + 1) * width])
    for step in range(1, n_dp):
        peer = lax.rem(me_dp + step, n_dp)
        start(send(g_send.at[peer], g_recv.at[me_dp], g_s.at[step], g_r.at[me_dp], dp=peer))
    g_recv[me_dp] = g_send[me_dp]

    for h in range(MINE):
        send(dq_send.at[h], dq_recv.at[h], dq_s.at[h], dq_r.at[h], ctx=nbr).wait_recv()
        dq_out[0, :, lanes((MINE * other + h) * heads, heads)] = dq_recv[h]

    for step in range(1, n_dp):
        src = lax.rem(me_dp + step, n_dp)
        send(g_send.at[src], g_recv.at[src], g_s.at[step], g_r.at[src], dp=src).wait_recv()
    part = g_recv[0].astype(F32)
    for d in range(1, n_dp):
        part = part + g_recv[d].astype(F32)
    c_recv[me] = part.astype(BF16)
    for step in range(1, n_ctx):
        peer = lax.rem(me + step, n_ctx)
        start(send(c_recv.at[me], c_recv.at[me], c_s.at[step], c_r.at[me], ctx=peer))
    for step in range(1, n_ctx):
        src = lax.rem(me + step, n_ctx)
        send(c_recv.at[src], c_recv.at[src], c_s.at[step], c_r.at[src], ctx=src).wait_recv()
    whole = c_recv[0].astype(F32)
    for c in range(1, n_ctx):
        whole = whole + c_recv[c].astype(F32)
    grad_own = jnp.concatenate([whole[: whole.shape[0] // 2], whole[whole.shape[0] // 2 :]], axis=1)
    squares = jnp.sum(grad_own * grad_own, axis=(0, 1), keepdims=True)
    sq_recv[me_dp] = jnp.broadcast_to(squares, sq_recv.shape[1:])
    for step in range(1, n_dp):
        peer = lax.rem(me_dp + step, n_dp)
        start(send(sq_recv.at[me_dp], sq_recv.at[me_dp], sq_s.at[step], sq_r.at[me_dp], dp=peer))
    for step in range(1, n_dp):
        src = lax.rem(me_dp + step, n_dp)
        send(sq_recv.at[src], sq_recv.at[src], sq_s.at[step], sq_r.at[src], dp=src).wait_recv()
    total_sq = sq_recv[0]
    for d in range(1, n_dp):
        total_sq = total_sq + sq_recv[d]
    clip = jnp.minimum(1.0, 1.0 / jnp.sqrt(total_sq + 1e-06))[0:1, 0:1]
    scaled = grad_own * clip
    moment = 0.9 * m1_v[...] + 0.1 * scaled
    second = 0.999 * m2_v[...] + 0.001 * scaled * scaled
    step_out[...] = moment / BIAS_ONE / (jnp.sqrt(second / BIAS_TWO) + 1e-08)

    for copy in sends:
        copy.wait_send()
    for h in range(MINE):
        for dest in range(n_z):
            for way in range(2):
                @pl.when((dest > z if way == 0 else dest < z))
                def _(dest=dest, way=way):
                    d_copy(h, dest, way).wait_send()

                @pl.when((dest <= z if way == 0 else dest >= z) & has_next(way))
                def _(dest=dest, way=way):
                    for part in range(2):
                        z_copy(h, part, dest, way).wait_send()


def per_device(n_dp, n_ctx, *args):
    args = list(args)
    args[7] = jnp.swapaxes(args[7], 1, 2)
    adapter = args[8]
    rank, width = adapter.shape
    n_z = n_ctx // 2
    hbm = pl.BlockSpec(memory_space=pl.ANY)
    heads = GROUP * DH
    stack = 2 * GROUP * ROWS
    dma = pltpu.SemaphoreType.DMA
    vmem = pl.BlockSpec(memory_space=pltpu.VMEM)
    fold = (2 * rank, width // 2)
    return pl.pallas_call(
        functools.partial(kernel, n_dp, n_ctx),
        out_shape=(
            jax.ShapeDtypeStruct((1, ROWS, H * DH), BF16),
            jax.ShapeDtypeStruct((1, ROWS, 2 * KVH * DH), BF16),
            jax.ShapeDtypeStruct((rank, width), F32),
        ),
        in_specs=[pl.BlockSpec(memory_space=pltpu.SMEM)] + [hbm] * 10,
        out_specs=(vmem, vmem, vmem),
        scratch_shapes=[
            pltpu.VMEM((MINE, n_z, 2, 2 * ROWS, DH), BF16),
            pltpu.VMEM((2, H, ROWS), F32),
            pltpu.VMEM((H, ROWS), F32),
            pltpu.VMEM((MINE, stack, DH), BF16),
            pltpu.VMEM((MINE, stack, DH), BF16),
            pltpu.VMEM((MINE, 1, stack), F32),
            pltpu.VMEM((MINE, 1, stack), F32),
            pltpu.VMEM((MINE, DH, stack), F32),
            pltpu.VMEM((MINE, n_z, 2, 2 * ROWS, DH), BF16),
            pltpu.VMEM((MINE, 2, n_z, 2, 2 * ROWS, DH), BF16),
            pltpu.VMEM((MINE, ROWS, heads), BF16),
            pltpu.VMEM((MINE, ROWS, heads), BF16),
            pltpu.VMEM((MINE, 2, ROWS, DH), BF16),
            pltpu.VMEM((MINE, 2, ROWS, DH), BF16),
            pltpu.VMEM((n_dp, rank, width), F32),
            pltpu.VMEM((n_dp,) + fold, BF16),
            pltpu.VMEM((n_dp,) + fold, BF16),
            pltpu.VMEM((n_ctx,) + fold, BF16),
            pltpu.VMEM((n_dp, 8, 128), F32),
            pltpu.VMEM((ROWS, D), BF16),
            pltpu.VMEM((ROWS, H * DH), BF16),
            pltpu.VMEM((ROWS, H * DH), BF16),
            pltpu.VMEM((H, ROWS), F32),
            pltpu.VMEM((rank, width), F32),
            pltpu.VMEM((rank, width), F32),
            dma((MINE, 2)), dma((MINE, 2)),
            dma((MINE, 2, GROUP)), dma((MINE, 2, GROUP)),
            dma((1,)), dma((1,)),
            dma((MINE, 2, 2, n_z)), dma((MINE, 2, n_z)),
            dma((MINE, n_z)), dma((MINE, 2, n_z)),
            dma((MINE,)), dma((MINE,)),
            dma((MINE,)), dma((MINE,)),
            dma((n_dp,)), dma((n_dp,)),
            dma((n_dp,)), dma((n_dp,)),
            dma((n_ctx,)), dma((n_ctx,)),
            dma((n_dp,)), dma((n_dp,)),
            dma((MINE, 2)), dma((MINE, 2, GROUP)), dma((7,)),
        ],
        compiler_params=pltpu.CompilerParams(
            collective_id=0, has_side_effects=True, vmem_limit_bytes=60 * 2**20
        ),
        cost_estimate=pl.CostEstimate(flops=3 * 10**9, bytes_accessed=4 * 2**20, transcendentals=2**21),
    )(*args)


def solution(mesh):
    rows = P("dp", "ctx", None)
    columns = P(None, "dp")
    return jax.shard_map(
        functools.partial(per_device, mesh.shape["dp"], mesh.shape["ctx"]),
        mesh=mesh,
        in_specs=(P("dp", None),) + (rows,) * 7 + (columns,) * 3,
        out_specs=(rows, rows, columns),
        check_vma=False,
    )
```

```python
import functools

import jax
import jax.numpy as jnp
from jax import lax
from jax.experimental import pallas as pl
from jax.experimental.pallas import tpu as pltpu
from jax.sharding import PartitionSpec as P

D = 4096
H = 16
KVH = 4
DH = 128
ROWS = 128
HALF = 64
GROUP = H // KVH
MINE = KVH // 2
CHUNK = 2 * ROWS
SCALE = DH ** (-0.5)
LOG2E = 1.4426950408889634
BIAS_ONE = 1.0 - 0.9**100.0
BIAS_TWO = 1.0 - 0.999**100.0
F32 = jnp.float32
BF16 = jnp.bfloat16


def dot_nn(a, b):
    return jnp.dot(a, b, preferred_element_type=F32)


def dot_nt(a, b):
    return lax.dot_general(a, b, (((1,), (1,)), ((), ())), preferred_element_type=F32)


def dot_tn(a, b):
    return lax.dot_general(a, b, (((0,), (0,)), ((), ())), preferred_element_type=F32)


def lanes(start, width):
    return pl.ds(pl.multiple_of(start, DH), width)


def send(src, dst, send_sem, recv_sem, **target):
    return pltpu.make_async_remote_copy(
        src_ref=src,
        dst_ref=dst,
        send_sem=send_sem,
        recv_sem=recv_sem,
        device_id=target,
        device_id_type=pl.DeviceIdType.MESH,
    )


def kernel(
    n_dp, n_ctx,
    span_ref, hid_ref, q_ref, k_ref, v_ref, o_ref, do_ref, ln_ref, ad_ref, m1_ref, m2_ref,
    dq_out, kv_out, step_out,
    kv_all, stat, stat_nbr, q_own, q_nbr, do_nbr, ln_row, de_row, dq_t,
    d_send, d_recv, d_pass, dq_send, dq_recv, kx_send, kx_recv,
    ad_all, g_send, g_recv, c_recv, sq_recv,
    hid_v, o_v, do_v, ln_v, m1_v, m2_v,
    xk_s, xk_r, xq_s, xq_r, st_s, st_r, z_s, z_r, d_s, d_r, p_r, dq_s, dq_r, kx_s, kx_r,
    ad_s, ad_r, g_s, g_r, c_s, c_r, sq_s, sq_r, l_kv, l_q, l_s,
):
    me_dp = lax.axis_index("dp")
    me = lax.axis_index("ctx")
    n_z = n_ctx // 2
    z, x = me // 2, lax.rem(me, 2)
    other = 1 - x
    nbr = 2 * z + other
    width = ad_ref.shape[1]
    fold = width // 2
    per = H // 2
    heads = GROUP * DH
    sources = (k_ref, v_ref)
    sends = []

    def start(copy):
        copy.start()
        sends.append(copy)

    def row_half(part):
        return pl.ds(pl.multiple_of(part * ROWS, ROWS), ROWS)

    own_kv = [
        [
            pltpu.make_async_copy(
                sources[w].at[0, :, lanes((MINE * x + h) * DH, DH)],
                kv_all.at[h, z, w, row_half(x), :],
                l_kv.at[h, w],
            )
            for w in range(2)
        ]
        for h in range(MINE)
    ]
    own_q = [pltpu.make_async_copy(q_ref.at[0, :, lanes(x * per * DH, per * DH)], q_own, l_q.at[0])]
    own_rest = [
        pltpu.make_async_copy(src, dst, l_s.at[i])
        for i, (src, dst) in enumerate((
            (do_ref.at[0], do_v), (o_ref.at[0], o_v), (ln_ref.at[0], ln_v),
            (ad_ref, ad_all.at[me_dp]), (hid_ref.at[0], hid_v), (m1_ref, m1_v), (m2_ref, m2_v),
        ))
    ]
    for copy in own_kv[0] + own_kv[1] + own_rest[:4] + own_q + own_rest[4:]:
        copy.start()

    barrier = pltpu.get_barrier_semaphore()
    for step in range(1, n_ctx):
        pl.semaphore_signal(barrier, inc=1, device_id={"ctx": lax.rem(me + step, n_ctx)},
                            device_id_type=pl.DeviceIdType.MESH)
    for step in range(1, n_dp):
        pl.semaphore_signal(barrier, inc=1, device_id={"dp": lax.rem(me_dp + step, n_dp)},
                            device_id_type=pl.DeviceIdType.MESH)
    for copy in own_rest[:4]:
        copy.wait()
    for part in range(2):
        stat[part, 0:per, :] = ln_v[part * per : (part + 1) * per, :]
    for head in range(H):
        cols = slice(head * DH, (head + 1) * DH)
        prod = do_v[:, cols].astype(F32) * o_v[:, cols].astype(F32)
        at = per + head % per
        stat[head // per, at : at + 1, :] = jnp.sum(prod.T, axis=0, keepdims=True)
    pl.semaphore_wait(barrier, n_ctx - 1 + n_dp - 1)

    def x_kv(h, w, part):
        return send(
            sources[w].at[0, :, lanes((MINE * other + h) * DH, DH)],
            kv_all.at[h, z, w, row_half(part), :],
            xk_s.at[h, w], xk_r.at[h, w], ctx=nbr,
        )

    def x_q(h, w):
        src, dst = ((q_ref, q_nbr), (do_ref, do_nbr))[w]
        cols = lanes((MINE * other + h) * heads, heads)
        return send(src.at[0, :, cols], dst.at[h], xq_s.at[h, w], xq_r.at[h, w], ctx=nbr)

    def z_at(way, reach):
        return z + reach if way == 0 else z - reach

    def has_z(way, reach):
        return z + reach < n_z if way == 0 else z >= reach

    def z_copy(h, part, owner, way, reach=1):
        rows = row_half(x if part == 0 else other)
        return send(
            kv_all.at[h, owner, :, rows, :], kv_all.at[h, owner, :, rows, :],
            z_s.at[h, part, way, reach - 1, owner], z_r.at[h, part, owner],
            ctx=2 * z_at(way, reach) + x,
        )

    def z_push(h, part):
        for reach in (2, 1):
            for way in range(2):
                @pl.when(has_z(way, reach))
                def _(way=way, reach=reach):
                    z_copy(h, part, z, way, reach).start()

    def z_take(h, distance):
        for part in range(2):
            for way in range(2):
                owner = z - distance if way == 0 else z + distance

                @pl.when((owner >= 0) & (owner < n_z))
                def _(part=part, way=way, owner=owner):
                    z_copy(h, part, owner, way).wait_recv()
                    if distance > 1:
                        @pl.when(has_z(way, 1))
                        def _():
                            z_copy(h, part, owner, way).start()

    for h in range(MINE):
        for w in range(2):
            start(x_kv(h, w, x))
    for copy in own_kv[0]:
        copy.wait()
    z_push(0, 0)
    for w in range(2):
        start(x_q(0, w))
    for step in range(1, n_dp):
        peer = lax.rem(me_dp + step, n_dp)
        start(send(ad_ref, ad_all.at[me_dp], ad_s.at[step], ad_r.at[me_dp], dp=peer))

    start(send(stat.at[other], stat_nbr, st_s.at[0], st_r.at[0], ctx=nbr))
    for w in range(2):
        start(x_q(1, w))

    for w in range(2):
        x_kv(0, w, other).wait_recv()
    z_push(0, 1)
    for copy in own_kv[1]:
        copy.wait()
    z_push(1, 0)
    for w in range(2):
        x_kv(1, w, other).wait_recv()
    z_push(1, 1)
    z_take(0, 2)

    for reach in range(1, 3):
        for way in range(2):
            @pl.when(jnp.logical_not(has_z(1 - way, reach)))
            def _(way=way, reach=reach):
                for h in range(MINE):
                    d_recv[h, way, reach - 1] = jnp.zeros(d_recv.shape[3:], BF16)

    for copy in own_rest[4:] + own_q:
        copy.wait()
    for step in range(1, n_dp):
        src = lax.rem(me_dp + step, n_dp)
        send(ad_ref, ad_all.at[src], ad_s.at[step], ad_r.at[src], dp=src).wait_recv()
    adapter_low = jnp.concatenate([ad_all[d] for d in range(n_dp)], axis=1).astype(BF16)
    mixed_down = dot_nt(adapter_low[:, :D], hid_v[...]).astype(BF16)

    z_take(0, 1)
    for distance in range(3, n_z):
        z_take(0, distance)

    send(stat.at[other], stat_nbr, st_s.at[0], st_r.at[0], ctx=nbr).wait_recv()
    for h in range(MINE):
        for g in range(GROUP):
            at = h * GROUP + g
            own = slice(g * ROWS, (g + 1) * ROWS)
            far = slice((GROUP + g) * ROWS, (GROUP + g + 1) * ROWS)
            ln_row[h, :, own] = stat[x, at : at + 1, :] * LOG2E
            ln_row[h, :, far] = stat_nbr[at : at + 1, :] * LOG2E
            de_row[h, :, own] = stat[x, per + at : per + at + 1, :]
            de_row[h, :, far] = stat_nbr[per + at : per + at + 1, :]

    lane_row = lax.broadcasted_iota(jnp.int32, (1, ROWS), 1)
    key_row = lax.broadcasted_iota(jnp.int32, (HALF, ROWS), 0)

    def query_pos(device):
        first, second = span_ref[0, 2 * device], span_ref[0, 2 * device + 1]
        return jnp.where(lane_row < HALF, first * HALF + lane_row, second * HALF + lane_row - HALF)

    pos_own, pos_far = query_pos(me), query_pos(nbr)
    chunks = 2 * GROUP * ROWS // CHUNK

    def d_near(h, dest, way, reach):
        return send(d_send.at[h, dest], d_recv.at[h, way, reach - 1], d_s.at[h, dest],
                    d_r.at[h, way, reach - 1], ctx=2 * z_at(way, reach) + x)

    def d_far(h, dest, way):
        return send(d_send.at[h, dest], d_pass.at[h, dest], d_s.at[h, dest],
                    p_r.at[h, dest], ctx=2 * z_at(way, 1) + x)

    def d_start(h, dest, way, gap):
        for reach in range(1, 3):
            @pl.when(gap == reach)
            def _(reach=reach):
                d_near(h, dest, way, reach).start()

        @pl.when(gap > 2)
        def _():
            d_far(h, dest, way).start()

    def hops(h, step):
        for way in range(2):
            before = z if way == 0 else n_z - 1 - z
            turn = step - (before - 1)
            dest = n_z - 1 - turn if way == 0 else turn
            gap = dest - z if way == 0 else z - dest

            @pl.when((before > 0) & (turn >= 0) & (gap > 1))
            def _(way=way, dest=dest, gap=gap):
                d_far(h, dest, way).wait_recv()
                both = d_send[h, dest].astype(F32) + d_pass[h, dest].astype(F32)
                d_send[h, dest] = both.astype(BF16)
                d_start(h, dest, way, gap)

    def dq_finish(h):
        for g in range(GROUP):
            far = slice((GROUP + g) * ROWS, (GROUP + g + 1) * ROWS)
            dq_send[h, :, g * DH : (g + 1) * DH] = (dq_t[h, :, far].T * SCALE).astype(BF16)
        start(send(dq_send.at[h], dq_recv.at[h], dq_s.at[h], dq_r.at[h], ctx=nbr))
        for g in range(GROUP):
            own = slice(g * ROWS, (g + 1) * ROWS)
            dq_out[0, :, lanes((x * per + h * GROUP + g) * DH, DH)] = (
                dq_t[h, :, own].T * SCALE
            ).astype(BF16)

    pair = CHUNK // ROWS

    def query_rows(h, j):
        if j < chunks // 2:
            at = [(h * GROUP + j * pair + i) * DH for i in range(pair)]
            q_rows = [q_own[:, a : a + DH] for a in at]
            do_rows = [do_v[:, lanes(x * per * DH + a, DH)] for a in at]
        else:
            at = [((j - chunks // 2) * pair + i) * DH for i in range(pair)]
            q_rows = [q_nbr[h, :, a : a + DH] for a in at]
            do_rows = [do_nbr[h, :, a : a + DH] for a in at]
        return jnp.concatenate(q_rows, axis=0), jnp.concatenate(do_rows, axis=0)

    for h in range(MINE):
        for w in range(2):
            x_q(h, w).wait_recv()
        dq_t[h] = jnp.zeros(dq_t.shape[1:], F32)

        def block(step, carry, h=h):
            t = jnp.where(lax.rem(step, 2) == 0, n_z - 1 - step // 2, step // 2)
            keys, values = kv_all[h, t, 0], kv_all[h, t, 1]
            keys_t = keys.T
            pos_key = jnp.concatenate(
                [span_ref[0, 4 * t + s] * HALF + key_row for s in range(4)], axis=0
            )
            hidden_from = [
                jnp.where(pos_key <= pos, 0.0, -jnp.inf).astype(F32) for pos in (pos_own, pos_far)
            ]
            dk = jnp.zeros((2 * ROWS, DH), F32)
            dv = jnp.zeros((2 * ROWS, DH), F32)
            for j in range(chunks):
                cols = slice(j * CHUNK, (j + 1) * CHUNK)
                q_rows, do_rows = query_rows(h, j)
                mask = hidden_from[2 * j // chunks]
                mask = jnp.concatenate([mask] * (CHUNK // ROWS), axis=1)
                scores = dot_nt(keys, q_rows) * (SCALE * LOG2E)
                weights = jnp.exp2(scores - ln_row[h, :, cols] + mask)
                d_weights = dot_nt(values, do_rows)
                d_scores = (weights * (d_weights - de_row[h, :, cols])).astype(BF16)
                dv = dv + dot_nn(weights.astype(BF16), do_rows)
                dk = dk + dot_nn(d_scores, q_rows)
                dq_t[h, :, cols] += dot_nn(keys_t, d_scores)
            d_send[h, t, 0] = (dk * SCALE).astype(BF16)
            d_send[h, t, 1] = dv.astype(BF16)

            for way in range(2):
                gap = t - z if way == 0 else z - t
                first = z == 0 if way == 0 else z == n_z - 1

                @pl.when((gap == 1) | ((gap > 1) & first))
                def _(way=way, gap=gap):
                    d_start(h, t, way, gap)

            if h == 0:
                @pl.when(step == 0)
                def _():
                    z_take(1, 2)

            @pl.when((step > 0) & (lax.rem(step, 2) == 0))
            def _():
                hops(h, step // 2 - 1)

            return carry

        lax.fori_loop(0, n_z, block, 0)
        for step in range((n_z + 1) // 2 - 1, n_z - 3):
            hops(h, step)
        if h == 0:
            z_take(1, 1)
            for distance in range(3, n_z):
                z_take(1, distance)
        if h == 0:
            dq_finish(0)

    kv_width = KVH * DH

    def finish(h):
        for way in range(2):
            for reach in range(1, 3):
                @pl.when(has_z(1 - way, reach))
                def _(way=way, reach=reach):
                    d_near(h, z, way, reach).wait_recv()
        for w in range(2):
            def total(rows):
                acc = d_send[h, z, w, rows, :].astype(F32)
                for way in range(2):
                    for reach in range(2):
                        acc = acc + d_recv[h, way, reach, w, rows, :].astype(F32)
                return acc.astype(BF16)

            kx_send[h, w] = total(row_half(other))
            kv_out[0, :, lanes(w * kv_width + (MINE * x + h) * DH, DH)] = total(row_half(x))
        start(send(kx_send.at[h], kx_recv.at[h], kx_s.at[h], kx_r.at[h], ctx=nbr))

    finish(0)
    dq_finish(1)
    finish(1)
    for h in range(MINE):
        send(kx_send.at[h], kx_recv.at[h], kx_s.at[h], kx_r.at[h], ctx=nbr).wait_recv()
        for w in range(2):
            kv_out[0, :, lanes(w * kv_width + (MINE * other + h) * DH, DH)] = kx_recv[h, w]

    kv_low = kv_out[0]
    mixed_up = dot_nt(adapter_low[:, D:], kv_low).astype(BF16)
    grad = jnp.concatenate([dot_nn(mixed_up, hid_v[...]), dot_nn(mixed_down, kv_low)], axis=1)

    def folded(block):
        return jnp.concatenate([block[:, :fold], block[:, fold:]], axis=0).astype(BF16)

    for d in range(n_dp):
        g_send[d] = folded(grad[:, d * width : (d + 1) * width])
    for step in range(1, n_dp):
        peer = lax.rem(me_dp + step, n_dp)
        start(send(g_send.at[peer], g_recv.at[me_dp], g_s.at[step], g_r.at[me_dp], dp=peer))
    g_recv[me_dp] = g_send[me_dp]

    for h in range(MINE):
        send(dq_send.at[h], dq_recv.at[h], dq_s.at[h], dq_r.at[h], ctx=nbr).wait_recv()
        dq_out[0, :, lanes((MINE * other + h) * heads, heads)] = dq_recv[h]

    for step in range(1, n_dp):
        src = lax.rem(me_dp + step, n_dp)
        send(g_send.at[src], g_recv.at[src], g_s.at[step], g_r.at[src], dp=src).wait_recv()
    part = g_recv[0].astype(F32)
    for d in range(1, n_dp):
        part = part + g_recv[d].astype(F32)
    c_recv[me] = part.astype(BF16)
    for step in range(1, n_ctx):
        peer = lax.rem(me + step, n_ctx)
        start(send(c_recv.at[me], c_recv.at[me], c_s.at[step], c_r.at[me], ctx=peer))
    for step in range(1, n_ctx):
        src = lax.rem(me + step, n_ctx)
        send(c_recv.at[src], c_recv.at[src], c_s.at[step], c_r.at[src], ctx=src).wait_recv()
    whole = c_recv[0].astype(F32)
    for c in range(1, n_ctx):
        whole = whole + c_recv[c].astype(F32)
    grad_own = jnp.concatenate([whole[: whole.shape[0] // 2], whole[whole.shape[0] // 2 :]], axis=1)
    squares = jnp.sum(grad_own * grad_own, axis=(0, 1), keepdims=True)
    sq_recv[me_dp] = jnp.broadcast_to(squares, sq_recv.shape[1:])
    for step in range(1, n_dp):
        peer = lax.rem(me_dp + step, n_dp)
        start(send(sq_recv.at[me_dp], sq_recv.at[me_dp], sq_s.at[step], sq_r.at[me_dp], dp=peer))
    for step in range(1, n_dp):
        src = lax.rem(me_dp + step, n_dp)
        send(sq_recv.at[src], sq_recv.at[src], sq_s.at[step], sq_r.at[src], dp=src).wait_recv()
    total_sq = sq_recv[0]
    for d in range(1, n_dp):
        total_sq = total_sq + sq_recv[d]
    clip = jnp.minimum(1.0, 1.0 / jnp.sqrt(total_sq + 1e-06))[0:1, 0:1]
    scaled = grad_own * clip
    moment = 0.9 * m1_v[...] + 0.1 * scaled
    second = 0.999 * m2_v[...] + 0.001 * scaled * scaled
    step_out[...] = moment / BIAS_ONE / (jnp.sqrt(second / BIAS_TWO) + 1e-08)

    for copy in sends:
        copy.wait_send()
    for h in range(MINE):
        for dest in range(n_z):
            for way in range(2):
                @pl.when((dest > z if way == 0 else dest < z))
                def _(dest=dest, way=way):
                    d_far(h, dest, way).wait_send()

                @pl.when((dest <= z - 2 if way == 0 else dest >= z + 2) & has_z(way, 1))
                def _(dest=dest, way=way):
                    for part in range(2):
                        z_copy(h, part, dest, way).wait_send()

        for reach in range(1, 3):
            for way in range(2):
                @pl.when(has_z(way, reach))
                def _(reach=reach, way=way):
                    for part in range(2):
                        z_copy(h, part, z, way, reach).wait_send()


def per_device(n_dp, n_ctx, *args):
    args = list(args)
    args[7] = jnp.swapaxes(args[7], 1, 2)
    adapter = args[8]
    rank, width = adapter.shape
    n_z = n_ctx // 2
    hbm = pl.BlockSpec(memory_space=pl.ANY)
    heads = GROUP * DH
    stack = 2 * GROUP * ROWS
    dma = pltpu.SemaphoreType.DMA
    vmem = pl.BlockSpec(memory_space=pltpu.VMEM)
    fold = (2 * rank, width // 2)
    return pl.pallas_call(
        functools.partial(kernel, n_dp, n_ctx),
        out_shape=(
            jax.ShapeDtypeStruct((1, ROWS, H * DH), BF16),
            jax.ShapeDtypeStruct((1, ROWS, 2 * KVH * DH), BF16),
            jax.ShapeDtypeStruct((rank, width), F32),
        ),
        in_specs=[pl.BlockSpec(memory_space=pltpu.SMEM)] + [hbm] * 10,
        out_specs=(vmem, vmem, vmem),
        scratch_shapes=[
            pltpu.VMEM((MINE, n_z, 2, 2 * ROWS, DH), BF16),
            pltpu.VMEM((2, H, ROWS), F32),
            pltpu.VMEM((H, ROWS), F32),
            pltpu.VMEM((ROWS, H // 2 * DH), BF16),
            pltpu.VMEM((MINE, ROWS, heads), BF16),
            pltpu.VMEM((MINE, ROWS, heads), BF16),
            pltpu.VMEM((MINE, 1, stack), F32),
            pltpu.VMEM((MINE, 1, stack), F32),
            pltpu.VMEM((MINE, DH, stack), F32),
            pltpu.VMEM((MINE, n_z, 2, 2 * ROWS, DH), BF16),
            pltpu.VMEM((MINE, 2, 2, 2, 2 * ROWS, DH), BF16),
            pltpu.VMEM((MINE, n_z, 2, 2 * ROWS, DH), BF16),
            pltpu.VMEM((MINE, ROWS, heads), BF16),
            pltpu.VMEM((MINE, ROWS, heads), BF16),
            pltpu.VMEM((MINE, 2, ROWS, DH), BF16),
            pltpu.VMEM((MINE, 2, ROWS, DH), BF16),
            pltpu.VMEM((n_dp, rank, width), F32),
            pltpu.VMEM((n_dp,) + fold, BF16),
            pltpu.VMEM((n_dp,) + fold, BF16),
            pltpu.VMEM((n_ctx,) + fold, BF16),
            pltpu.VMEM((n_dp, 8, 128), F32),
            pltpu.VMEM((ROWS, D), BF16),
            pltpu.VMEM((ROWS, H * DH), BF16),
            pltpu.VMEM((ROWS, H * DH), BF16),
            pltpu.VMEM((H, ROWS), F32),
            pltpu.VMEM((rank, width), F32),
            pltpu.VMEM((rank, width), F32),
            dma((MINE, 2)), dma((MINE, 2)),
            dma((MINE, 2)), dma((MINE, 2)),
            dma((1,)), dma((1,)),
            dma((MINE, 2, 2, 2, n_z)), dma((MINE, 2, n_z)),
            dma((MINE, n_z)), dma((MINE, 2, 2)), dma((MINE, n_z)),
            dma((MINE,)), dma((MINE,)),
            dma((MINE,)), dma((MINE,)),
            dma((n_dp,)), dma((n_dp,)),
            dma((n_dp,)), dma((n_dp,)),
            dma((n_ctx,)), dma((n_ctx,)),
            dma((n_dp,)), dma((n_dp,)),
            dma((MINE, 2)), dma((1,)), dma((7,)),
        ],
        compiler_params=pltpu.CompilerParams(
            collective_id=0, has_side_effects=True, vmem_limit_bytes=60 * 2**20
        ),
        cost_estimate=pl.CostEstimate(flops=3 * 10**9, bytes_accessed=4 * 2**20, transcendentals=2**21),
    )(*args)


def solution(mesh):
    rows = P("dp", "ctx", None)
    columns = P(None, "dp")
    return jax.shard_map(
        functools.partial(per_device, mesh.shape["dp"], mesh.shape["ctx"]),
        mesh=mesh,
        in_specs=(P("dp", None),) + (rows,) * 7 + (columns,) * 3,
        out_specs=(rows, rows, columns),
        check_vma=False,
    )
```

```python
import functools

import jax
import jax.numpy as jnp
from jax import lax
from jax.experimental import pallas as pl
from jax.experimental.pallas import tpu as pltpu
from jax.sharding import PartitionSpec as P

D = 4096
H = 16
KVH = 4
DH = 128
ROWS = 128
HALF = 64
GROUP = H // KVH
MINE = KVH // 2
CHUNK = 2 * ROWS
SCALE = DH ** (-0.5)
LOG2E = 1.4426950408889634
BIAS_ONE = 1.0 - 0.9**100.0
BIAS_TWO = 1.0 - 0.999**100.0
F32 = jnp.float32
BF16 = jnp.bfloat16


def dot_nn(a, b):
    return jnp.dot(a, b, preferred_element_type=F32)


def dot_nt(a, b):
    return lax.dot_general(a, b, (((1,), (1,)), ((), ())), preferred_element_type=F32)


def dot_tn(a, b):
    return lax.dot_general(a, b, (((0,), (0,)), ((), ())), preferred_element_type=F32)


def lanes(start, width):
    return pl.ds(pl.multiple_of(start, DH), width)


def send(src, dst, send_sem, recv_sem, **target):
    return pltpu.make_async_remote_copy(
        src_ref=src,
        dst_ref=dst,
        send_sem=send_sem,
        recv_sem=recv_sem,
        device_id=target,
        device_id_type=pl.DeviceIdType.MESH,
    )


def kernel(
    n_dp, n_ctx,
    span_ref, hid_ref, q_ref, k_ref, v_ref, o_ref, do_ref, ln_ref, ad_ref, m1_ref, m2_ref,
    dq_out, kv_out, step_out,
    kv_all, stat, stat_nbr, q_st, do_st, ln_row, de_row, dq_t,
    d_send, d_recv, dq_send, dq_recv, kx_send, kx_recv,
    ad_all, g_send, g_recv, c_recv, sq_recv,
    hid_v, o_v, do_v, ln_v, m1_v, m2_v,
    xk_s, xk_r, xq_s, xq_r, st_s, st_r, z_s, z_r, d_s, d_r, dq_s, dq_r, kx_s, kx_r,
    ad_s, ad_r, g_s, g_r, c_s, c_r, sq_s, sq_r, l_kv, l_q, l_s,
):
    me_dp = lax.axis_index("dp")
    me = lax.axis_index("ctx")
    n_z = n_ctx // 2
    z, x = me // 2, lax.rem(me, 2)
    other = 1 - x
    nbr = 2 * z + other
    width = ad_ref.shape[1]
    fold = width // 2
    per = H // 2
    heads = GROUP * DH
    sources = (k_ref, v_ref)
    sends = []

    def start(copy):
        copy.start()
        sends.append(copy)

    def row_half(part):
        return pl.ds(pl.multiple_of(part * ROWS, ROWS), ROWS)

    own_kv = [
        [
            pltpu.make_async_copy(
                sources[w].at[0, :, lanes((MINE * x + h) * DH, DH)],
                kv_all.at[h, z, w, row_half(x), :],
                l_kv.at[h, w],
            )
            for w in range(2)
        ]
        for h in range(MINE)
    ]
    own_q = [
        pltpu.make_async_copy(
            src.at[0, :, lanes((x * per + h * GROUP + g) * DH, DH)],
            dst.at[h, g * ROWS : (g + 1) * ROWS, :],
            l_q.at[h, w, g],
        )
        for h in range(MINE)
        for w, (src, dst) in enumerate(((q_ref, q_st), (do_ref, do_st)))
        for g in range(GROUP)
    ]
    own_rest = [
        pltpu.make_async_copy(src, dst, l_s.at[i])
        for i, (src, dst) in enumerate((
            (do_ref.at[0], do_v), (o_ref.at[0], o_v), (ln_ref.at[0], ln_v),
            (ad_ref, ad_all.at[me_dp]), (hid_ref.at[0], hid_v), (m1_ref, m1_v), (m2_ref, m2_v),
        ))
    ]
    for copy in own_kv[0] + own_kv[1] + own_rest[:4] + own_q + own_rest[4:]:
        copy.start()

    barrier = pltpu.get_barrier_semaphore()
    def greet(device):
        pl.semaphore_signal(barrier, inc=1, device_id={"ctx": device},
                            device_id_type=pl.DeviceIdType.MESH)

    greet(nbr)
    for way in range(2):
        @pl.when(z < n_z - 1 if way == 0 else z > 0)
        def _(way=way):
            greet(me + 2 if way == 0 else me - 2)

    for step in range(1, n_dp):
        pl.semaphore_signal(barrier, inc=1, device_id={"dp": lax.rem(me_dp + step, n_dp)},
                            device_id_type=pl.DeviceIdType.MESH)
    for copy in own_rest[:4]:
        copy.wait()
    for part in range(2):
        stat[part, 0:per, :] = ln_v[part * per : (part + 1) * per, :]
    for head in range(H):
        cols = slice(head * DH, (head + 1) * DH)
        prod = do_v[:, cols].astype(F32) * o_v[:, cols].astype(F32)
        at = per + head % per
        stat[head // per, at : at + 1, :] = jnp.sum(prod.T, axis=0, keepdims=True)
    ends = jnp.where(z == 0, 1, 0) + jnp.where(z == n_z - 1, 1, 0)
    pl.semaphore_wait(barrier, n_dp + 2 - ends)

    def x_kv(h, w, part):
        return send(
            sources[w].at[0, :, lanes((MINE * other + h) * DH, DH)],
            kv_all.at[h, z, w, row_half(part), :],
            xk_s.at[h, w], xk_r.at[h, w], ctx=nbr,
        )

    def x_q(h, w, g):
        src, dst = ((q_ref, q_st), (do_ref, do_st))[w]
        return send(
            src.at[0, :, lanes((other * per + h * GROUP + g) * DH, DH)],
            dst.at[h, (GROUP + g) * ROWS : (GROUP + g + 1) * ROWS, :],
            xq_s.at[h, w, g], xq_r.at[h, w, g], ctx=nbr,
        )

    def next_z(way):
        return z + 1 if way == 0 else z - 1

    def has_next(way):
        return z < n_z - 1 if way == 0 else z > 0

    def z_copy(h, part, owner, way):
        rows = row_half(x if part == 0 else other)
        return send(
            kv_all.at[h, owner, :, rows, :], kv_all.at[h, owner, :, rows, :],
            z_s.at[h, part, way, owner], z_r.at[h, part, owner], ctx=2 * next_z(way) + x,
        )

    def z_push(h, part):
        for way in range(2):
            @pl.when(has_next(way))
            def _(way=way):
                z_copy(h, part, z, way).start()

    def z_relay(h, distance):
        for part in range(2):
            for way in range(2):
                owner = z - distance if way == 0 else z + distance

                @pl.when((owner >= 0) & (owner < n_z))
                def _(part=part, way=way, owner=owner):
                    z_copy(h, part, owner, way).wait_recv()

                    @pl.when(has_next(way))
                    def _():
                        z_copy(h, part, owner, way).start()

    for h in range(MINE):
        for w in range(2):
            start(x_kv(h, w, x))
    for copy in own_kv[0]:
        copy.wait()
    z_push(0, 0)
    for w in range(2):
        for g in range(GROUP):
            start(x_q(0, w, g))
    for step in range(1, n_dp):
        peer = lax.rem(me_dp + step, n_dp)
        start(send(ad_ref, ad_all.at[me_dp], ad_s.at[step], ad_r.at[me_dp], dp=peer))

    start(send(stat.at[other], stat_nbr, st_s.at[0], st_r.at[0], ctx=nbr))
    for w in range(2):
        for g in range(GROUP):
            start(x_q(1, w, g))

    for w in range(2):
        x_kv(0, w, other).wait_recv()
    z_push(0, 1)
    for distance in range(1, n_z - 1):
        z_relay(0, distance)
    for copy in own_kv[1]:
        copy.wait()
    z_push(1, 0)
    for w in range(2):
        x_kv(1, w, other).wait_recv()
    z_push(1, 1)

    @pl.when(z == 0)
    def _():
        for h in range(MINE):
            d_recv[h, 0, z] = jnp.zeros(d_recv.shape[3:], BF16)

    @pl.when(z == n_z - 1)
    def _():
        for h in range(MINE):
            d_recv[h, 1, z] = jnp.zeros(d_recv.shape[3:], BF16)

    for copy in own_rest[4:] + own_q:
        copy.wait()
    for step in range(1, n_dp):
        src = lax.rem(me_dp + step, n_dp)
        send(ad_ref, ad_all.at[src], ad_s.at[step], ad_r.at[src], dp=src).wait_recv()
    adapter_low = jnp.concatenate([ad_all[d] for d in range(n_dp)], axis=1).astype(BF16)
    mixed_down = dot_nt(adapter_low[:, :D], hid_v[...]).astype(BF16)

    z_relay(0, n_z - 1)

    send(stat.at[other], stat_nbr, st_s.at[0], st_r.at[0], ctx=nbr).wait_recv()
    for h in range(MINE):
        for g in range(GROUP):
            at = h * GROUP + g
            own = slice(g * ROWS, (g + 1) * ROWS)
            far = slice((GROUP + g) * ROWS, (GROUP + g + 1) * ROWS)
            ln_row[h, :, own] = stat[x, at : at + 1, :] * LOG2E
            ln_row[h, :, far] = stat_nbr[at : at + 1, :] * LOG2E
            de_row[h, :, own] = stat[x, per + at : per + at + 1, :]
            de_row[h, :, far] = stat_nbr[per + at : per + at + 1, :]

    lane_row = lax.broadcasted_iota(jnp.int32, (1, ROWS), 1)
    key_row = lax.broadcasted_iota(jnp.int32, (HALF, ROWS), 0)

    def query_pos(device):
        first, second = span_ref[0, 2 * device], span_ref[0, 2 * device + 1]
        return jnp.where(lane_row < HALF, first * HALF + lane_row, second * HALF + lane_row - HALF)

    pos_own, pos_far = query_pos(me), query_pos(nbr)
    chunks = 2 * GROUP * ROWS // CHUNK

    def d_copy(h, dest, way):
        return send(d_send.at[h, dest], d_recv.at[h, way, dest], d_s.at[h, dest],
                    d_r.at[h, way, dest], ctx=2 * next_z(way) + x)

    def hops(h, step, lag):
        for way in range(2):
            before = z if way == 0 else n_z - 1 - z
            turn = step - lag * (before - 1)
            dest = n_z - 1 - turn if way == 0 else turn
            ahead = dest > z if way == 0 else dest < z

            @pl.when((before > 0) & (turn >= 0) & ahead)
            def _(way=way, dest=dest):
                d_copy(h, dest, way).wait_recv()
                both = d_send[h, dest].astype(F32) + d_recv[h, way, dest].astype(F32)
                d_send[h, dest] = both.astype(BF16)
                d_copy(h, dest, way).start()

    def dq_finish(h):
        for g in range(GROUP):
            far = slice((GROUP + g) * ROWS, (GROUP + g + 1) * ROWS)
            dq_send[h, :, g * DH : (g + 1) * DH] = (dq_t[h, :, far].T * SCALE).astype(BF16)
        start(send(dq_send.at[h], dq_recv.at[h], dq_s.at[h], dq_r.at[h], ctx=nbr))
        for g in range(GROUP):
            own = slice(g * ROWS, (g + 1) * ROWS)
            dq_out[0, :, lanes((x * per + h * GROUP + g) * DH, DH)] = (
                dq_t[h, :, own].T * SCALE
            ).astype(BF16)

    for h in range(MINE):
        for w in range(2):
            for g in range(GROUP):
                x_q(h, w, g).wait_recv()
        dq_t[h] = jnp.zeros(dq_t.shape[1:], F32)

        def block(step, carry, h=h):
            t = jnp.where(lax.rem(step, 2) == 0, n_z - 1 - step // 2, step // 2)
            keys, values = kv_all[h, t, 0], kv_all[h, t, 1]
            keys_t = keys.T
            pos_key = jnp.concatenate(
                [span_ref[0, 4 * t + s] * HALF + key_row for s in range(4)], axis=0
            )
            hidden_from = [
                jnp.where(pos_key <= pos, 0.0, -jnp.inf).astype(F32) for pos in (pos_own, pos_far)
            ]
            dk = jnp.zeros((2 * ROWS, DH), F32)
            dv = jnp.zeros((2 * ROWS, DH), F32)
            for j in range(chunks):
                cols = slice(j * CHUNK, (j + 1) * CHUNK)
                q_rows, do_rows = q_st[h, cols, :], do_st[h, cols, :]
                mask = hidden_from[2 * j // chunks]
                mask = jnp.concatenate([mask] * (CHUNK // ROWS), axis=1)
                scores = dot_nt(keys, q_rows) * (SCALE * LOG2E)
                weights = jnp.exp2(scores - ln_row[h, :, cols] + mask)
                d_weights = dot_nt(values, do_rows)
                d_scores = (weights * (d_weights - de_row[h, :, cols])).astype(BF16)
                dv = dv + dot_nn(weights.astype(BF16), do_rows)
                dk = dk + dot_nn(d_scores, q_rows)
                dq_t[h, :, cols] += dot_nn(keys_t, d_scores)
            d_send[h, t, 0] = (dk * SCALE).astype(BF16)
            d_send[h, t, 1] = dv.astype(BF16)

            @pl.when((z == 0) & (t > z))
            def _():
                d_copy(h, t, 0).start()

            @pl.when((z == n_z - 1) & (t < z))
            def _():
                d_copy(h, t, 1).start()

            if h == 0:
                @pl.when(step > 0)
                def _():
                    z_relay(1, step)
            else:
                hops(0, step, 2)

                @pl.when((step > 0) & (lax.rem(step, 2) == 0))
                def _():
                    hops(1, step // 2 - 1, 1)

            return carry

        lax.fori_loop(0, n_z, block, 0)

        if h == 0:
            dq_finish(0)

    for step in range(n_z, 2 * n_z - 5):
        hops(0, step, 2)

    kv_width = KVH * DH

    def finish(h):
        for way in range(2):
            @pl.when(z > 0 if way == 0 else z < n_z - 1)
            def _(way=way):
                d_copy(h, z, way).wait_recv()
        for w in range(2):
            def total(rows):
                acc = d_send[h, z, w, rows, :].astype(F32)
                for way in range(2):
                    acc = acc + d_recv[h, way, z, w, rows, :].astype(F32)
                return acc.astype(BF16)

            kx_send[h, w] = total(row_half(other))
            kv_out[0, :, lanes(w * kv_width + (MINE * x + h) * DH, DH)] = total(row_half(x))
        start(send(kx_send.at[h], kx_recv.at[h], kx_s.at[h], kx_r.at[h], ctx=nbr))

    for step in range((n_z + 1) // 2 - 1, n_z - 2):
        hops(1, step, 1)
    finish(0)
    dq_finish(1)
    finish(1)
    for h in range(MINE):
        send(kx_send.at[h], kx_recv.at[h], kx_s.at[h], kx_r.at[h], ctx=nbr).wait_recv()
        for w in range(2):
            kv_out[0, :, lanes(w * kv_width + (MINE * other + h) * DH, DH)] = kx_recv[h, w]

    kv_low = kv_out[0]
    mixed_up = dot_nt(adapter_low[:, D:], kv_low).astype(BF16)
    grad = jnp.concatenate([dot_nn(mixed_up, hid_v[...]), dot_nn(mixed_down, kv_low)], axis=1)

    def folded(block):
        return jnp.concatenate([block[:, :fold], block[:, fold:]], axis=0).astype(BF16)

    for d in range(n_dp):
        g_send[d] = folded(grad[:, d * width : (d + 1) * width])
    for step in range(1, n_dp):
        peer = lax.rem(me_dp + step, n_dp)
        start(send(g_send.at[peer], g_recv.at[me_dp], g_s.at[step], g_r.at[me_dp], dp=peer))
    g_recv[me_dp] = g_send[me_dp]

    for h in range(MINE):
        send(dq_send.at[h], dq_recv.at[h], dq_s.at[h], dq_r.at[h], ctx=nbr).wait_recv()
        dq_out[0, :, lanes((MINE * other + h) * heads, heads)] = dq_recv[h]

    for step in range(1, n_dp):
        src = lax.rem(me_dp + step, n_dp)
        send(g_send.at[src], g_recv.at[src], g_s.at[step], g_r.at[src], dp=src).wait_recv()
    part = g_recv[0].astype(F32)
    for d in range(1, n_dp):
        part = part + g_recv[d].astype(F32)
    c_recv[me] = part.astype(BF16)
    for step in range(1, n_ctx):
        peer = lax.rem(me + step, n_ctx)
        start(send(c_recv.at[me], c_recv.at[me], c_s.at[step], c_r.at[me], ctx=peer))
    for step in range(1, n_ctx):
        src = lax.rem(me + step, n_ctx)
        send(c_recv.at[src], c_recv.at[src], c_s.at[step], c_r.at[src], ctx=src).wait_recv()
    whole = c_recv[0].astype(F32)
    for c in range(1, n_ctx):
        whole = whole + c_recv[c].astype(F32)
    grad_own = jnp.concatenate([whole[: whole.shape[0] // 2], whole[whole.shape[0] // 2 :]], axis=1)
    squares = jnp.sum(grad_own * grad_own, axis=(0, 1), keepdims=True)
    sq_recv[me_dp] = jnp.broadcast_to(squares, sq_recv.shape[1:])
    for step in range(1, n_dp):
        peer = lax.rem(me_dp + step, n_dp)
        start(send(sq_recv.at[me_dp], sq_recv.at[me_dp], sq_s.at[step], sq_r.at[me_dp], dp=peer))
    for step in range(1, n_dp):
        src = lax.rem(me_dp + step, n_dp)
        send(sq_recv.at[src], sq_recv.at[src], sq_s.at[step], sq_r.at[src], dp=src).wait_recv()
    total_sq = sq_recv[0]
    for d in range(1, n_dp):
        total_sq = total_sq + sq_recv[d]
    clip = jnp.minimum(1.0, 1.0 / jnp.sqrt(total_sq + 1e-06))[0:1, 0:1]
    scaled = grad_own * clip
    moment = 0.9 * m1_v[...] + 0.1 * scaled
    second = 0.999 * m2_v[...] + 0.001 * scaled * scaled
    step_out[...] = moment / BIAS_ONE / (jnp.sqrt(second / BIAS_TWO) + 1e-08)

    for copy in sends:
        copy.wait_send()
    for h in range(MINE):
        for dest in range(n_z):
            for way in range(2):
                @pl.when((dest > z if way == 0 else dest < z))
                def _(dest=dest, way=way):
                    d_copy(h, dest, way).wait_send()

                @pl.when((dest <= z if way == 0 else dest >= z) & has_next(way))
                def _(dest=dest, way=way):
                    for part in range(2):
                        z_copy(h, part, dest, way).wait_send()


def per_device(n_dp, n_ctx, *args):
    args = list(args)
    args[7] = jnp.swapaxes(args[7], 1, 2)
    adapter = args[8]
    rank, width = adapter.shape
    n_z = n_ctx // 2
    hbm = pl.BlockSpec(memory_space=pl.ANY)
    heads = GROUP * DH
    stack = 2 * GROUP * ROWS
    dma = pltpu.SemaphoreType.DMA
    vmem = pl.BlockSpec(memory_space=pltpu.VMEM)
    fold = (2 * rank, width // 2)
    return pl.pallas_call(
        functools.partial(kernel, n_dp, n_ctx),
        out_shape=(
            jax.ShapeDtypeStruct((1, ROWS, H * DH), BF16),
            jax.ShapeDtypeStruct((1, ROWS, 2 * KVH * DH), BF16),
            jax.ShapeDtypeStruct((rank, width), F32),
        ),
        in_specs=[pl.BlockSpec(memory_space=pltpu.SMEM)] + [hbm] * 10,
        out_specs=(vmem, vmem, vmem),
        scratch_shapes=[
            pltpu.VMEM((MINE, n_z, 2, 2 * ROWS, DH), BF16),
            pltpu.VMEM((2, H, ROWS), F32),
            pltpu.VMEM((H, ROWS), F32),
            pltpu.VMEM((MINE, stack, DH), BF16),
            pltpu.VMEM((MINE, stack, DH), BF16),
            pltpu.VMEM((MINE, 1, stack), F32),
            pltpu.VMEM((MINE, 1, stack), F32),
            pltpu.VMEM((MINE, DH, stack), F32),
            pltpu.VMEM((MINE, n_z, 2, 2 * ROWS, DH), BF16),
            pltpu.VMEM((MINE, 2, n_z, 2, 2 * ROWS, DH), BF16),
            pltpu.VMEM((MINE, ROWS, heads), BF16),
            pltpu.VMEM((MINE, ROWS, heads), BF16),
            pltpu.VMEM((MINE, 2, ROWS, DH), BF16),
            pltpu.VMEM((MINE, 2, ROWS, DH), BF16),
            pltpu.VMEM((n_dp, rank, width), F32),
            pltpu.VMEM((n_dp,) + fold, BF16),
            pltpu.VMEM((n_dp,) + fold, BF16),
            pltpu.VMEM((n_ctx,) + fold, BF16),
            pltpu.VMEM((n_dp, 8, 128), F32),
            pltpu.VMEM((ROWS, D), BF16),
            pltpu.VMEM((ROWS, H * DH), BF16),
            pltpu.VMEM((ROWS, H * DH), BF16),
            pltpu.VMEM((H, ROWS), F32),
            pltpu.VMEM((rank, width), F32),
            pltpu.VMEM((rank, width), F32),
            dma((MINE, 2)), dma((MINE, 2)),
            dma((MINE, 2, GROUP)), dma((MINE, 2, GROUP)),
            dma((1,)), dma((1,)),
            dma((MINE, 2, 2, n_z)), dma((MINE, 2, n_z)),
            dma((MINE, n_z)), dma((MINE, 2, n_z)),
            dma((MINE,)), dma((MINE,)),
            dma((MINE,)), dma((MINE,)),
            dma((n_dp,)), dma((n_dp,)),
            dma((n_dp,)), dma((n_dp,)),
            dma((n_ctx,)), dma((n_ctx,)),
            dma((n_dp,)), dma((n_dp,)),
            dma((MINE, 2)), dma((MINE, 2, GROUP)), dma((7,)),
        ],
        compiler_params=pltpu.CompilerParams(
            collective_id=0, has_side_effects=True, vmem_limit_bytes=60 * 2**20
        ),
        cost_estimate=pl.CostEstimate(flops=3 * 10**9, bytes_accessed=4 * 2**20, transcendentals=2**21),
    )(*args)


def solution(mesh):
    rows = P("dp", "ctx", None)
    columns = P(None, "dp")
    return jax.shard_map(
        functools.partial(per_device, mesh.shape["dp"], mesh.shape["ctx"]),
        mesh=mesh,
        in_specs=(P("dp", None),) + (rows,) * 7 + (columns,) * 3,
        out_specs=(rows, rows, columns),
        check_vma=False,
    )
```
